256 devices in a mesh: docs: 32 (over z_hi, x, core), heads: 8 (over z_lo, y).
Axes of the slice: x: 4, y: 4, z: 8 (z_hi: 4, z_lo: 2; z = z_hi * 2 + z_lo), core: 2. Of those that a mesh axis runs over, the one named last changes fastest.
Arguments:
- queries: bfloat16 [16384, 4096], P('docs', 'heads'), may hold values from -6 to 6
- keys: bfloat16 [16384, 2048], P('docs', 'heads'), may hold values from -6 to 6
- values: bfloat16 [16384, 2048], P('docs', 'heads'), may hold values from -6 to 6
- prefix_keys: bfloat16 [2048, 2048], P('docs', 'heads'), may hold values from -6 to 6
- prefix_values: bfloat16 [2048, 2048], P('docs', 'heads'), may hold values from -6 to 6
- out_grad: bfloat16 [16384, 4608], P('docs', 'heads'), may hold values from -24 to 24
- out_weight: bfloat16 [4096, 4608], P('heads'), may hold values from -0.09375 to 0.09375
- doc_lengths: int32 [32, 3], P('docs'), may hold values from 1 to 256, 512 in all within a row
Outputs:
- query_grad: bfloat16 [16384, 4096], P('docs', 'heads')
- key_grad: bfloat16 [16384, 2048], P('docs', 'heads')
- value_grad: bfloat16 [16384, 2048], P('docs', 'heads')
- prefix_key_grad: bfloat16 [2048, 2048], P('docs', 'heads')
- prefix_value_grad: bfloat16 [2048, 2048], P('docs', 'heads')
The draws below stay inside these ranges and needn't reach their ends.
Inputs may be any that keep to these rules, and one draw needn't show every extreme that they name: Each row of doc_lengths sums to 512, and its largest entry is exactly 256.
All inputs are finite; a program needn't handle non-finite values.
Results may differ from the reference program's by a relative error of at most 0.02.
Values may be sent and summed in bfloat16 or wider, within the bound.
A program may use at most 128 MiB of HBM per device.

```python
import math
import jax
import jax.numpy as jnp
import numpy as np
from jax import lax

D = 4608
HEADS = 32
KV_HEADS = 16
HEAD_DIM = 128
PREFIX = 2048
TOK_DEV = 512
DOCS_DEV = 3
DOC_MOST = 256
DOC_GROUPS = 32
TOKENS = 16384


def levels(rng, extent, split, least, largest):
    def one(axis_at, parts):
        draws = jax.random.uniform(jax.random.fold_in(jax.random.fold_in(rng, 6), axis_at), (parts,), jnp.float32, least / len(split), largest / len(split))
        return jnp.repeat(jnp.exp(draws), extent[axis_at] // parts).reshape((-1,) + (1,) * (len(extent) - axis_at - 1))

    factor_of = one(*split[0])
    for cut in split[1:]:
        factor_of = factor_of * one(*cut)
    return factor_of


def profile(count, total, reach, slope):
    loads = [(1 << 20) // math.isqrt(standing ** slope) + 1 for standing in range(2, count + 1)]
    surplus, counts = total - reach - (count - 1), [1] * (count - 1)
    while surplus > 0:
        candidates = [i for i in range(count - 1) if counts[i] < reach]
        pool, budget = sum([loads[i] for i in candidates]), surplus
        for i in candidates:
            more = min(reach - counts[i], max(1, budget * loads[i] // pool), surplus)
            counts[i] = counts[i] + more
            surplus = surplus - more
    return np.array([reach] + counts)


def ragged(rng, count, total, reach, slope):
    if count == 2:
        one = jax.random.randint(rng, (), max(1, total - reach), min(reach, total - 1) + 1)
        return jnp.stack([one, total - one])
    sizes = jnp.asarray(profile(count, total, reach, slope), jnp.int32)
    twos = (count - 1) // 2
    donor, receiver = sizes[1:1 + 2 * twos:2], sizes[2:2 + 2 * twos:2]
    room = jnp.minimum(donor - 1, reach - receiver)
    shifted = jax.random.randint(jax.random.fold_in(rng, 1), (twos,), 0, 1 << 20) % (room + 1)
    sizes = sizes.at[1:1 + 2 * twos:2].set(donor - shifted).at[2:2 + 2 * twos:2].set(receiver + shifted)
    return sizes[jax.random.permutation(jax.random.fold_in(rng, 2), count)]


def normal_values(own_key, dims, spread, reach, pieces=(), kind=jnp.bfloat16):
    drawn = spread * jax.random.normal(own_key, dims, jnp.float32)
    if pieces:
        drawn = drawn * levels(own_key, dims, pieces, -0.22, 0.18)
    return jnp.clip(drawn, -reach, reach).astype(kind)


def setup_inputs(seed: int = 0) -> dict:
    splits = jax.random.split(jax.random.key(seed), 9)
    queries = normal_values(splits[0], (TOKENS, HEADS * HEAD_DIM), 1.0, 6.0, ((0, 32), (1, 8)))
    keys = normal_values(splits[1], (TOKENS, KV_HEADS * HEAD_DIM), 1.0, 6.0, ((0, 32), (1, 8)))
    values = normal_values(splits[2], (TOKENS, KV_HEADS * HEAD_DIM), 1.0, 6.0, ((0, 32), (1, 8)))
    prefix_keys = normal_values(splits[3], (PREFIX, KV_HEADS * HEAD_DIM), 1.0, 6.0, ((0, 32), (1, 8)))
    prefix_values = normal_values(splits[4], (PREFIX, KV_HEADS * HEAD_DIM), 1.0, 6.0, ((0, 32), (1, 8)))
    out_grad = normal_values(splits[5], (TOKENS, D), 4.0, 24.0, ((0, 32), (1, 8)))
    out_weight = normal_values(splits[6], (HEADS * HEAD_DIM, D), (HEADS * HEAD_DIM) ** -0.5, 0.09375, ((0, 8),))
    doc_lengths = jax.vmap(lambda own: ragged(own, DOCS_DEV, TOK_DEV, DOC_MOST, 2))(jax.random.split(splits[7], DOC_GROUPS)).reshape((DOC_GROUPS, DOCS_DEV)).astype(jnp.int32)
    return {"queries": queries, "keys": keys, "values": values, "prefix_keys": prefix_keys, "prefix_values": prefix_values, "out_grad": out_grad, "out_weight": out_weight, "doc_lengths": doc_lengths}


softcap = 50.0
query_scale = 1.0 / 12.0


def doc_mask(lengths, count):
    bounds = jnp.cumsum(lengths).astype(jnp.int32)
    position = jnp.arange(count, dtype=jnp.int32)
    segment = jnp.sum((position[:, None] >= bounds[None, :]).astype(jnp.int32), axis=1)
    return (segment[:, None] == segment[None, :]) & (position[None, :] <= position[:, None])


def capped(raw):
    return softcap * jnp.tanh(raw * (query_scale / softcap))


def group_terms(query, key, value, grad, pkey, pvalue, lengths):
    fl = jnp.float32
    tok = query.shape[0]
    group = HEADS // KV_HEADS
    qrows = query.reshape(tok, KV_HEADS, group, HEAD_DIM).astype(fl)
    dout = grad.reshape(tok, KV_HEADS, group, HEAD_DIM).astype(fl)
    krows = key.reshape(tok, KV_HEADS, HEAD_DIM).astype(fl)
    vrows = value.reshape(tok, KV_HEADS, HEAD_DIM).astype(fl)
    pkrows = pkey.reshape(PREFIX, KV_HEADS, HEAD_DIM).astype(fl)
    pvrows = pvalue.reshape(PREFIX, KV_HEADS, HEAD_DIM).astype(fl)
    mask = doc_mask(lengths, tok)
    s_pre = capped(jnp.einsum('tkgd,pkd->kgtp', qrows, pkrows))
    s_doc = capped(jnp.einsum('tkgd,jkd->kgtj', qrows, krows))
    e_pre = jnp.exp(s_pre)
    e_doc = jnp.where(mask, jnp.exp(s_doc), jnp.float32(0.0))
    total = jnp.sum(e_pre, axis=-1, keepdims=True) + jnp.sum(e_doc, axis=-1, keepdims=True)
    p_pre = e_pre / total
    p_doc = e_doc / total
    b_pre = p_pre.astype(jnp.bfloat16).astype(fl)
    b_doc = p_doc.astype(jnp.bfloat16).astype(fl)
    attn_out = jnp.einsum('kgtp,pkd->tkgd', b_pre, pvrows) + jnp.einsum('kgtj,jkd->tkgd', b_doc, vrows)
    delta = jnp.einsum('tkgd,tkgd->kgt', dout, attn_out)[..., None]
    dp_pre = jnp.einsum('tkgd,pkd->kgtp', dout, pvrows)
    dp_doc = jnp.einsum('tkgd,jkd->kgtj', dout, vrows)
    l_pre = (p_pre * (dp_pre - delta) * (1.0 - (s_pre / softcap) * (s_pre / softcap)) * query_scale).astype(jnp.bfloat16).astype(fl)
    l_doc = (p_doc * (dp_doc - delta) * (1.0 - (s_doc / softcap) * (s_doc / softcap)) * query_scale).astype(jnp.bfloat16).astype(fl)
    dq = jnp.einsum('kgtp,pkd->tkgd', l_pre, pkrows) + jnp.einsum('kgtj,jkd->tkgd', l_doc, krows)
    dk = jnp.einsum('kgtj,tkgd->jkd', l_doc, qrows)
    dv = jnp.einsum('kgtj,tkgd->jkd', b_doc, dout)
    pdk = jnp.einsum('kgtp,tkgd->pkd', l_pre, qrows).reshape(PREFIX, KV_HEADS * HEAD_DIM)
    pdv = jnp.einsum('kgtp,tkgd->pkd', b_pre, dout).reshape(PREFIX, KV_HEADS * HEAD_DIM)
    return (dq.reshape(tok, HEADS * HEAD_DIM).astype(jnp.bfloat16),
            dk.reshape(tok, KV_HEADS * HEAD_DIM).astype(jnp.bfloat16),
            dv.reshape(tok, KV_HEADS * HEAD_DIM).astype(jnp.bfloat16), pdk, pdv)


def reference(queries, keys, values, prefix_keys, prefix_values, out_grad, out_weight, doc_lengths):
    head_grad = jnp.dot(out_grad, out_weight.T, preferred_element_type=jnp.float32).astype(jnp.bfloat16)
    q_all = queries.reshape(DOC_GROUPS, TOK_DEV, HEADS * HEAD_DIM)
    k_all = keys.reshape(DOC_GROUPS, TOK_DEV, KV_HEADS * HEAD_DIM)
    v_all = values.reshape(DOC_GROUPS, TOK_DEV, KV_HEADS * HEAD_DIM)
    g_all = head_grad.reshape(DOC_GROUPS, TOK_DEV, HEADS * HEAD_DIM)

    def visit(carry, items):
        query, key, value, grad, lengths = items
        dq, dk, dv, pdk, pdv = group_terms(query, key, value, grad, prefix_keys, prefix_values, lengths)
        return (carry[0] + pdk, carry[1] + pdv), (dq, dk, dv)

    start = jnp.zeros((PREFIX, KV_HEADS * HEAD_DIM), jnp.float32)
    sums, grads = lax.scan(visit, (start, start), (q_all, k_all, v_all, g_all, doc_lengths))
    query_grad = grads[0].reshape(TOKENS, HEADS * HEAD_DIM)
    key_grad = grads[1].reshape(TOKENS, KV_HEADS * HEAD_DIM)
    value_grad = grads[2].reshape(TOKENS, KV_HEADS * HEAD_DIM)
    return (query_grad, key_grad, value_grad, sums[0].astype(jnp.bfloat16), sums[1].astype(jnp.bfloat16))
```

```python
import functools
import math

import jax
import jax.numpy as jnp
from jax import lax
from jax.experimental import pallas as pl
from jax.experimental.pallas import tpu as pltpu
from jax.sharding import PartitionSpec as P

HD = 128
SOFTCAP = 50.0
SCALE = 1.0 / 12.0
LOG2E = 1.4426950408889634
F32 = jnp.float32
BF16 = jnp.bfloat16
MESH = pl.DeviceIdType.MESH

TOK = 512
FEAT = 576
NC = 4
CH = TOK // NC
QW = 1024
CW = 256


def dot(a, b, dims=((1,), (0,))):
    return lax.dot_general(a, b, (dims, ((), ())), preferred_element_type=F32)


def kernel(
    len_ref, q_ref, k_ref, v_ref, pk_ref, pv_ref, og_ref, w_ref,
    dq_ref, dk_ref, dv_ref, pdk_ref, pdv_ref,
    gbuf, wraw, wt, kbuf, vbuf, ebuf, sbuf, edoc, sdoc, qt, qs, dot_t, dos, dqt, ot, lsum, drow, hg,
    pb, pr, xs, xr, acc, zs, zr,
    w_sem, gs, gr, kzs, kzr, kxs, kxr, kcs, kcr, ps, prs, xss, xrs, zss, zrs,
):
    d = lax.axis_index("docs")
    h = lax.axis_index("heads")
    core = lax.rem(d, 2)
    x = lax.rem(d // 2, 4)
    zh = d // 8
    zl = h // 4
    y = lax.rem(h, 4)

    def doc_id(zz, xx, cc):
        return {"docs": (lax.rem(zz, 4) * 4 + lax.rem(xx, 4)) * 2 + cc}

    def head_at(zz, yy):
        return zz * 4 + lax.rem(yy + 8, 4)

    peers = [doc_id(zh + r, x, core) for r in (1, 2, 3)]
    peers += [doc_id(zh, x + r, core) for r in (1, 2, 3)]
    peers += [doc_id(zh, x, 1 - core)]
    peers += [{"heads": head_at(zl, y + 1)}, {"heads": head_at(zl, y - 1)}, {"heads": head_at(1 - zl, y)}]

    wcopy = pltpu.make_async_copy(w_ref, wraw, w_sem)
    wcopy.start()

    barrier = pltpu.get_barrier_semaphore()
    for p in peers:
        pl.semaphore_signal(barrier, inc=1, device_id=p, device_id_type=MESH)
    pl.semaphore_wait(barrier, len(peers))

    started = []

    def remote(src, dst, ssem, rsem, device):
        return pltpu.make_async_remote_copy(
            src_ref=src, dst_ref=dst, send_sem=ssem, recv_sem=rsem, device_id=device, device_id_type=MESH
        )

    def send(*args):
        c = remote(*args)
        c.start()
        started.append(c)

    def g_route(kind, c):
        s = 1 if c % 2 == 0 else -1
        right, left = y + s, y - s
        return [
            (head_at(zl, y), head_at(zl, right), head_at(zl, left)),
            (head_at(zl, y), head_at(zl, left), head_at(zl, right)),
            (head_at(zl, y), head_at(1 - zl, y), head_at(1 - zl, y)),
            (head_at(1 - zl, y), head_at(zl, right), head_at(1 - zl, left)),
            (head_at(zl, right), head_at(zl, left), head_at(zl, y + 2)),
            (head_at(zl, right), head_at(1 - zl, y), head_at(1 - zl, right)),
            (head_at(1 - zl, left), head_at(zl, right), head_at(1 - zl, y + 2)),
        ][kind]

    def g_copy(kind, c, receive):
        slot, to, arrives = g_route(kind, c)
        rows = pl.ds(c * CH, CH)
        at = gbuf.at[arrives if receive else slot, rows]
        src = og_ref.at[rows] if kind < 3 and not receive else at
        return remote(src, at, gs.at[kind, c], gr.at[kind, c], {"heads": to})

    def g_send(kind, c):
        cp = g_copy(kind, c, False)
        cp.start()
        started.append(cp)

    def g_wait(kind, c):
        g_copy(kind, c, True).wait_recv()

    both = ((0, pk_ref, kbuf), (1, pv_ref, vbuf))
    for i, src, buf in both:
        for r in (1, 2, 3):
            send(src, buf.at[zh, x, core], kzs.at[i, r - 1], kzr.at[i, r - 1], doc_id(zh + r, x, core))
    for c in range(NC):
        for kind in range(3):
            g_send(kind, c)
    for i, src, buf in both:
        buf[zh, x, core] = src[...]

    for hd in range(4):
        blk = q_ref[:, hd * HD : (hd + 1) * HD]
        qs[hd // 2, (hd % 2) * TOK : (hd % 2 + 1) * TOK, :] = blk
        qt[hd // 2, :, (hd % 2) * TOK : (hd % 2 + 1) * TOK] = blk.T
    ot[...] = jnp.zeros_like(ot)
    lsum[...] = jnp.zeros_like(lsum)

    def forward(kk, vv, hk, put, mask=None):
        rows = kk.shape[0]
        for n in range(QW // CW):
            cols = slice(n * CW, (n + 1) * CW)
            t = jnp.tanh(dot(kk, qt[hk, :, cols]) * (SCALE / SOFTCAP))
            e = jnp.exp2(t * (SOFTCAP * LOG2E))
            if mask is not None:
                e = jnp.where(mask(n * CW), e, 0.0)
            lsum[hk, :, cols] += jnp.sum(e.reshape(rows // 8, 8, CW), axis=0)
            eb = e.astype(BF16)
            put(cols, eb, (e * (1.0 - t * t)).astype(BF16))
            ot[hk, :, cols] += dot(vv, eb, ((0,), (0,)))

    b0 = len_ref[0, 0]
    b1 = b0 + len_ref[0, 1]
    b2 = b1 + len_ref[0, 2]

    def segment(p):
        return (p >= b0).astype(jnp.int32) + (p >= b1).astype(jnp.int32) + (p >= b2).astype(jnp.int32)

    def doc_forward(i, carry):
        hk = i // 4
        j = lax.rem(i, 4)
        rows = pl.ds(pl.multiple_of(j * HD, HD), HD)
        lanes = pl.ds(pl.multiple_of(hk * HD, HD), HD)

        def mask(first):
            key = j * HD + lax.broadcasted_iota(jnp.int32, (HD, CW), 0)
            row = first % TOK + lax.broadcasted_iota(jnp.int32, (HD, CW), 1)
            return (key <= row) & (segment(key) == segment(row))

        def put(cols, eb, sb):
            edoc[hk, rows, cols] = eb
            sdoc[hk, rows, cols] = sb

        forward(k_ref[rows, lanes], v_ref[rows, lanes], hk, put, mask)
        return carry

    lax.fori_loop(0, 8, doc_forward, 0)

    for i, src, buf in both:
        for r in (1, 2, 3):
            remote(src, buf.at[lax.rem(zh - r + 4, 4), x, core], kzs.at[i, r - 1], kzr.at[i, r - 1], doc_id(zh + r, x, core)).wait_recv()
        mine = buf.at[:, x, core]
        for r in (1, 2, 3):
            send(mine, mine, kxs.at[i, r - 1], kxr.at[i, r - 1], doc_id(zh, x + r, core))
        send(mine, mine, kcs.at[i, 0], kcr.at[i, 0], doc_id(zh, x, 1 - core))

    def g_forward(c):
        g_wait(2, c)
        g_send(3, c)
        g_wait(1, c)
        g_send(4, c)
        g_send(5, c)

    def g_last(c):
        g_wait(3, c)
        g_send(6, c)

    g_forward(0)
    g_forward(1)

    wcopy.wait()
    for i in range(4608 // HD):
        wt[i * HD : (i + 1) * HD, :] = wraw[:, i * HD : (i + 1) * HD].T

    g_forward(2)
    g_last(0)

    for i, src, buf in both:
        for r in (1, 2, 3):
            at = buf.at[:, lax.rem(x - r + 4, 4), core]
            remote(at, at, kxs.at[i, r - 1], kxr.at[i, r - 1], doc_id(zh, x + r, core)).wait_recv()
            send(at, at, kcs.at[i, r], kcr.at[i, r], doc_id(zh, x, 1 - core))
    g_forward(3)
    g_last(1)
    for i, src, buf in both:
        for r in range(4):
            at = buf.at[:, lax.rem(x - r + 4, 4), 1 - core]
            remote(at, at, kcs.at[i, r], kcr.at[i, r], doc_id(zh, x, 1 - core)).wait_recv()

    def pre_forward(i, carry):
        hk = i // 4
        zz = lax.rem(i, 4)
        lanes = pl.ds(pl.multiple_of(hk * HD, HD), HD)
        for xx in range(2):
            kk = kbuf[zz, 2 * xx : 2 * xx + 2, :, :, lanes].reshape(256, HD)
            vv = vbuf[zz, 2 * xx : 2 * xx + 2, :, :, lanes].reshape(256, HD)

            def put(cols, eb, sb):
                ebuf[hk, zz, 2 * xx : 2 * xx + 2, :, cols] = eb.reshape(2, HD, CW)
                sbuf[hk, zz, 2 * xx : 2 * xx + 2, :, cols] = sb.reshape(2, HD, CW)

            forward(kk, vv, hk, put)
        return carry

    lax.fori_loop(0, 4, pre_forward, 0)
    g_last(2)
    g_last(3)
    lax.fori_loop(4, 8, pre_forward, 0)

    def w_rows(s):
        return wt[pl.ds(pl.multiple_of(s * FEAT, FEAT), FEAT), :]

    hg[...] = dot(og_ref[...], w_rows(h))
    for kind, waited in ((0, False), (1, True), (2, True), (3, True), (5, False), (4, False), (6, False)):
        for c in range(NC):
            if not waited:
                g_wait(kind, c)
            slot = g_route(kind, c)[2]
            rows = slice(c * CH, (c + 1) * CH)
            hg[rows, :] += dot(gbuf[slot, rows, :], w_rows(slot))

    dqt[...] = jnp.zeros_like(dqt)
    for hd in range(4):
        hk, cols = hd // 2, slice((hd % 2) * TOK, (hd % 2 + 1) * TOK)
        g_t = hg[:, hd * HD : (hd + 1) * HD].T.astype(BF16).astype(F32)
        inv = 1.0 / jnp.sum(lsum[hk, :, cols], axis=0, keepdims=True)
        scaled = (g_t * inv).astype(BF16)
        drow[hk, :, cols] = jnp.sum(g_t * ot[hk, :, cols], axis=0, keepdims=True) * (inv * inv)
        dot_t[hk, :, cols] = scaled
        dos[hk, cols, :] = scaled.astype(F32).T.astype(BF16)

    def backward(kk, vv, hk, get):
        dk = dv = None
        for n in range(QW // CW):
            cols = slice(n * CW, (n + 1) * CW)
            eb, sb = get(cols)
            dp = dot(vv, dot_t[hk, :, cols]) - drow[hk, :, cols]
            ds = (sb.astype(F32) * dp).astype(BF16)
            a = dot(ds, qs[hk, cols, :])
            b = dot(eb, dos[hk, cols, :])
            dk = a if dk is None else dk + a
            dv = b if dv is None else dv + b
            dqt[hk, :, cols] += dot(kk, ds, ((0,), (0,)))
        return dk * SCALE, dv

    def quarter(r):
        xx = lax.rem(x + r, 4)

        def one(i, carry):
            hk = i // 2
            zz = lax.rem(i, 2) * 2
            lanes = pl.ds(pl.multiple_of(hk * HD, HD), HD)
            kk = kbuf[pl.ds(zz, 2), xx, :, :, lanes].reshape(256, HD)
            vv = vbuf[pl.ds(zz, 2), xx, :, :, lanes].reshape(256, HD)

            def get(cols):
                eb = ebuf[hk, pl.ds(zz, 2), xx, :, cols].reshape(256, CW)
                sb = sbuf[hk, pl.ds(zz, 2), xx, :, cols].reshape(256, CW)
                return eb, sb

            dk, dv = backward(kk, vv, hk, get)
            dk = dk.astype(BF16).reshape(2, 2, 64, HD)
            dv = dv.astype(BF16).reshape(2, 2, 64, HD)
            for cc in range(2):
                pb[r, cc, 0, pl.ds(zz, 2), :, lanes] = dk[:, cc]
                pb[r, cc, 1, pl.ds(zz, 2), :, lanes] = dv[:, cc]
            return carry

        lax.fori_loop(0, 4, one, 0)
        send(pb.at[r, 1 - core], pr.at[r], ps.at[r], prs.at[r], doc_id(zh, x, 1 - core))

    def pair_sum(r):
        remote(pb.at[r, 1 - core], pr.at[r], ps.at[r], prs.at[r], doc_id(zh, x, 1 - core)).wait_recv()
        return pb[r, core].astype(F32) + pr[r].astype(F32)

    def x_send(r):
        xs[r - 1] = pair_sum(r).astype(BF16)
        send(xs.at[r - 1], xr.at[r - 1], xss.at[r - 1], xrs.at[r - 1], doc_id(zh, x + r, core))

    quarter(2)
    quarter(1)
    x_send(2)
    quarter(3)
    x_send(1)
    quarter(0)
    x_send(3)

    def doc_backward(i, carry):
        hk = i // 2
        rows = pl.ds(pl.multiple_of(lax.rem(i, 2) * 256, 256), 256)
        lanes = pl.ds(pl.multiple_of(hk * HD, HD), HD)

        def get(cols):
            return edoc[hk, rows, cols], sdoc[hk, rows, cols]

        dk, dv = backward(k_ref[rows, lanes], v_ref[rows, lanes], hk, get)
        dk_ref[rows, lanes] = dk.astype(BF16)
        dv_ref[rows, lanes] = dv.astype(BF16)
        return carry

    lax.fori_loop(0, 4, doc_backward, 0)
    acc[...] = pair_sum(0)
    for r in (2, 1, 3):
        remote(xs.at[r - 1], xr.at[r - 1], xss.at[r - 1], xrs.at[r - 1], doc_id(zh, x + r, core)).wait_recv()
        acc[...] += xr[r - 1].astype(F32)
    for r in (2, 1, 3):
        zs[r - 1] = acc[:, lax.rem(zh + r, 4)].astype(BF16)
        send(zs.at[r - 1], zr.at[r - 1], zss.at[r - 1], zrs.at[r - 1], doc_id(zh + r, x, core))
    for hd in range(4):
        cols = slice((hd % 2) * TOK, (hd % 2 + 1) * TOK)
        dq_ref[:, hd * HD : (hd + 1) * HD] = (dqt[hd // 2, :, cols] * SCALE).T.astype(BF16)
    total = acc[:, zh]
    for r in (2, 1, 3):
        remote(zs.at[r - 1], zr.at[r - 1], zss.at[r - 1], zrs.at[r - 1], doc_id(zh + r, x, core)).wait_recv()
        total = total + zr[r - 1].astype(F32)
    pdk_ref[...] = total[0].astype(BF16)
    pdv_ref[...] = total[1].astype(BF16)
    for c in started:
        c.wait_send()


def on_device(queries, keys, values, prefix_keys, prefix_values, out_grad, out_weight, doc_lengths):
    sd = jax.ShapeDtypeStruct
    vm = pl.BlockSpec(memory_space=pltpu.VMEM)
    dma = pltpu.SemaphoreType.DMA
    return pl.pallas_call(
        kernel,
        out_shape=(
            sd((TOK, 512), BF16),
            sd((TOK, 256), BF16),
            sd((TOK, 256), BF16),
            sd((64, 256), BF16),
            sd((64, 256), BF16),
        ),
        in_specs=[pl.BlockSpec(memory_space=pltpu.SMEM)] + [vm] * 6 + [pl.BlockSpec(memory_space=pl.ANY)],
        out_specs=(vm,) * 5,
        scratch_shapes=[
            pltpu.VMEM((8, TOK, FEAT), BF16),
            pltpu.VMEM((512, 4608), BF16),
            pltpu.VMEM((4608, 512), BF16),
            pltpu.VMEM((4, 4, 2, 64, 256), BF16),
            pltpu.VMEM((4, 4, 2, 64, 256), BF16),
            pltpu.VMEM((2, 4, 4, HD, QW), BF16),
            pltpu.VMEM((2, 4, 4, HD, QW), BF16),
            pltpu.VMEM((2, TOK, QW), BF16),
            pltpu.VMEM((2, TOK, QW), BF16),
            pltpu.VMEM((2, HD, QW), BF16),
            pltpu.VMEM((2, QW, HD), BF16),
            pltpu.VMEM((2, HD, QW), BF16),
            pltpu.VMEM((2, QW, HD), BF16),
            pltpu.VMEM((2, HD, QW), F32),
            pltpu.VMEM((2, HD, QW), F32),
            pltpu.VMEM((2, 8, QW), F32),
            pltpu.VMEM((2, 1, QW), F32),
            pltpu.VMEM((TOK, 512), F32),
            pltpu.VMEM((4, 2, 2, 4, 64, 256), BF16),
            pltpu.VMEM((4, 2, 4, 64, 256), BF16),
            pltpu.VMEM((3, 2, 4, 64, 256), BF16),
            pltpu.VMEM((3, 2, 4, 64, 256), BF16),
            pltpu.VMEM((2, 4, 64, 256), F32),
            pltpu.VMEM((3, 2, 64, 256), BF16),
            pltpu.VMEM((3, 2, 64, 256), BF16),
            dma,
            dma((7, NC)),
            dma((7, NC)),
            dma((2, 3)),
            dma((2, 3)),
            dma((2, 3)),
            dma((2, 3)),
            dma((2, 4)),
            dma((2, 4)),
            dma((4,)),
            dma((4,)),
            dma((3,)),
            dma((3,)),
            dma((3,)),
            dma((3,)),
        ],
        compiler_params=pltpu.CompilerParams(
            collective_id=0, has_side_effects=True, vmem_limit_bytes=60 * 1024 * 1024
        ),
    )(doc_lengths, queries, keys, values, prefix_keys, prefix_values, out_grad, out_weight)


def solution(mesh):
    return jax.shard_map(
        on_device,
        mesh=mesh,
        in_specs=(P("docs", "heads"),) * 6 + (P("heads", None), P("docs", None)),
        out_specs=(P("docs", "heads"),) * 5,
        check_vma=False,
    )
```

```python
import jax
import jax.numpy as jnp
from jax import lax
from jax.experimental import pallas as pl
from jax.experimental.pallas import tpu as pltpu
from jax.sharding import PartitionSpec as P

HD = 128
SOFTCAP = 50.0
SCALE = 1.0 / 12.0
LOG2E = 1.4426950408889634
F32 = jnp.float32
BF16 = jnp.bfloat16
MESH = pl.DeviceIdType.MESH

TOK = 512
FEAT = 576
WIN = 640
NC = 4
CH = TOK // NC
QW = 1024
PRE = 2048
QR = 512


def dot(a, b, dims=((1,), (0,))):
    return lax.dot_general(a, b, (dims, ((), ())), preferred_element_type=F32)


def kernel(
    len_ref, q_hbm, k_hbm, v_hbm, pk_hbm, pv_hbm, og_hbm, w_hbm,
    dq_hbm, dk_hbm, dv_hbm, pdk_hbm, pdv_hbm,
    qb, kd, vd, gbuf, wraw, kbuf, vbuf, ebuf, sbuf, edoc, sdoc, qt, qs, dot_t, dos, ot, lsum, drow, hgt,
    pb, pr, xs, xc, xr, tacc, zs, zr, odq, odk, odv, opk, opv,
    ls, gs, gr, kzs, kzr, kxs, kxr, kcs, kcr, ps, prs, xss, xrs, zss, zrs, osem,
):
    d = lax.axis_index("docs")
    h = lax.axis_index("heads")
    core = lax.rem(d, 2)
    x = lax.rem(d // 2, 4)
    zh = d // 8
    zl = h // 4
    y = lax.rem(h, 4)

    def doc_id(zz, xx, cc):
        return {"docs": (lax.rem(zz + 4, 4) * 4 + lax.rem(xx + 4, 4)) * 2 + cc}

    def head_id(zz, yy):
        return {"heads": zz * 4 + lax.rem(yy + 4, 4)}

    other = doc_id(zh, x, 1 - core)
    xdev = {1: doc_id(zh, x + 1, core), -1: doc_id(zh, x - 1, core)}
    zdev = {1: doc_id(zh + 1, x, core), 2: doc_id(zh + 2, x, core), 3: doc_id(zh + 3, x, core)}
    ydev = {1: head_id(zl, y + 1), -1: head_id(zl, y - 1)}
    pdev = head_id(1 - zl, y)

    barrier = pltpu.get_barrier_semaphore()
    peers = (other, xdev[1], xdev[-1], zdev[1], zdev[2], zdev[3], ydev[1], ydev[-1], pdev)
    for p in peers:
        pl.semaphore_signal(barrier, inc=1, device_id=p, device_id_type=MESH)

    def slot_of(ry, rl):
        return (ry % 4) * 2 + rl

    def pad_of(ry):
        return lax.rem(y + ry % 4, 2)

    def rows_of(ry):
        return pl.ds(pl.multiple_of(pad_of(ry) * (WIN - FEAT), WIN - FEAT), FEAT)

    local = [
        pltpu.make_async_copy(q_hbm, qb, ls.at[0]),
        pltpu.make_async_copy(k_hbm, kd, ls.at[1]),
        pltpu.make_async_copy(v_hbm, vd, ls.at[2]),
        pltpu.make_async_copy(pk_hbm, kbuf.at[0:64], ls.at[3]),
        pltpu.make_async_copy(pv_hbm, vbuf.at[0:64], ls.at[4]),
        pltpu.make_async_copy(og_hbm, gbuf.at[0, rows_of(0)], ls.at[5]),
        pltpu.make_async_copy(w_hbm, wraw, ls.at[6]),
    ]
    for c in local:
        c.start()
    pl.semaphore_wait(barrier, len(peers))

    started = []

    def remote(src, dst, ssem, rsem, device):
        return pltpu.make_async_remote_copy(
            src_ref=src, dst_ref=dst, send_sem=ssem, recv_sem=rsem, device_id=device, device_id_type=MESH
        )

    def send(*args):
        c = remote(*args)
        c.start()
        started.append(c)

    def landed(dst, ssem, rsem):
        remote(dst, dst, ssem, rsem, other).wait_recv()

    def g_route(kind, c):
        s = 1 if c % 2 == 0 else -1
        return [
            ((0, 0), ydev[s], (-s, 0)),
            ((0, 0), ydev[-s], (s, 0)),
            ((0, 0), pdev, (0, 1)),
            ((0, 1), ydev[s], (-s, 1)),
            ((s, 0), ydev[-s], (2, 0)),
            ((s, 0), pdev, (s, 1)),
            ((-s, 1), ydev[s], (2, 1)),
        ][kind]

    def g_at(where, c):
        return gbuf.at[slot_of(*where), rows_of(where[0]), pl.ds(c * CH, CH)]

    def g_send(kind, c):
        here, to, there = g_route(kind, c)
        at = gbuf.at[slot_of(*there), rows_of(here[0]), pl.ds(c * CH, CH)]
        src = og_hbm.at[:, pl.ds(c * CH, CH)] if kind < 3 else g_at(here, c)
        send(src, at, gs.at[kind, c], gr.at[kind, c], to)

    def g_wait(kind, c):
        landed(g_at(g_route(kind, c)[2], c), gs.at[kind, c], gr.at[kind, c])

    pre = ((0, kbuf, pk_hbm), (1, vbuf, pv_hbm))

    def z_rows(rz):
        return pl.ds(rz * 64, 64)

    def x_rows(rx, piece):
        return pl.ds(rx * QR + (0 if piece == 0 else 64), 64 if piece == 0 else 192)

    def c_rows(rx, rc):
        return pl.ds(rx * QR + rc * 256, 256)

    for i, buf, src in pre:
        send(src, buf.at[z_rows(3)], kzs.at[i, 0], kzr.at[i, 0], zdev[1])
        send(src, buf.at[z_rows(1)], kzs.at[i, 1], kzr.at[i, 1], zdev[3])
    for i, buf, src in pre:
        send(src, buf.at[x_rows(3, 0)], kxs.at[i, 0, 0], kxr.at[i, 0, 0], xdev[1])
        send(src, buf.at[x_rows(1, 0)], kxs.at[i, 0, 1], kxr.at[i, 0, 1], xdev[-1])
    for c in range(NC):
        g_send(0, c)
        g_send(1, c)
    g_send(2, 0)

    for ry in range(4):
        zero = pl.ds(pl.multiple_of((1 - pad_of(ry)) * FEAT, WIN - FEAT), WIN - FEAT)
        for rl in range(2):
            gbuf[slot_of(ry, rl), zero, :] = jnp.zeros((WIN - FEAT, TOK), BF16)
    for c in local[:3]:
        c.wait()
    for hd in range(4):
        blk = qb[:, hd * HD : (hd + 1) * HD]
        qs[hd // 2, (hd % 2) * TOK : (hd % 2 + 1) * TOK, :] = blk
        qt[hd // 2, :, (hd % 2) * TOK : (hd % 2 + 1) * TOK] = blk.T

    b0 = len_ref[0, 0]
    b1 = b0 + len_ref[0, 1]
    b2 = b1 + len_ref[0, 2]

    def segment(p):
        return (p >= b0).astype(jnp.int32) + (p >= b1).astype(jnp.int32) + (p >= b2).astype(jnp.int32)

    def weights(kk, hk, cols, mask):
        t = jnp.tanh(dot(kk, qt[hk, :, cols]) * (SCALE / SOFTCAP))
        e = jnp.exp2(t * (SOFTCAP * LOG2E))
        if mask is not None:
            e = jnp.where(mask, e, 0.0)
        return e, e * (1.0 - t * t)

    def partial_sums(e):
        return jnp.sum(e.reshape(e.shape[0] // 8, 8, e.shape[1]), axis=0)

    def doc_forward(hk):
        lsum[hk] = jnp.zeros((8, QW), F32)
        for j in range(4):
            rows = slice(j * HD, (j + 1) * HD)
            lo, hi = j * HD, min(TOK, (j + 3) * HD)
            key = lo + lax.broadcasted_iota(jnp.int32, (HD, hi - lo), 0)
            row = lo + lax.broadcasted_iota(jnp.int32, (HD, hi - lo), 1)
            mask = (key <= row) & (segment(key) == segment(row))
            for g in range(2):
                cols = slice(g * TOK + lo, g * TOK + hi)
                e, s = weights(kd[rows, hk * HD : (hk + 1) * HD], hk, cols, mask)
                lsum[hk, :, cols] += partial_sums(e)
                edoc[hk, rows, cols] = e.astype(BF16)
                sdoc[hk, rows, cols] = s.astype(BF16)
                for a, b in ((0, lo), (hi, TOK)):
                    if a < b:
                        edoc[hk, rows, g * TOK + a : g * TOK + b] = jnp.zeros((HD, b - a), BF16)
                        sdoc[hk, rows, g * TOK + a : g * TOK + b] = jnp.zeros((HD, b - a), BF16)

    def pre_forward(rx):
        def one(hk, carry):
            rows = slice(rx * QR, (rx + 1) * QR)
            lanes = pl.ds(pl.multiple_of(hk * HD, HD), HD)
            e, s = weights(kbuf[rows, lanes], hk, slice(None), None)
            lsum[hk] += partial_sums(e)
            ebuf[hk, rows, :] = e.astype(BF16)
            sbuf[hk, rows, :] = s.astype(BF16)
            return carry

        lax.fori_loop(0, 2, one, 0)

    def x_pass(piece):
        for i, buf, _ in pre:
            got, to = ((3, 1), (1, -1))[i]
            side = 0 if got == 3 else 1
            landed(buf.at[x_rows(got, piece)], kxs.at[i, piece, side], kxr.at[i, piece, side])
            send(buf.at[x_rows(got, piece)], buf.at[x_rows(2, piece)], kxs.at[i, piece, 2], kxr.at[i, piece, 2], xdev[to])

    def x_rest(piece):
        for i, buf, _ in pre:
            got = (1, 3)[i]
            side = 0 if got == 3 else 1
            landed(buf.at[x_rows(got, piece)], kxs.at[i, piece, side], kxr.at[i, piece, side])

    def x_across(piece):
        for i, buf, _ in pre:
            landed(buf.at[x_rows(2, piece)], kxs.at[i, piece, 2], kxr.at[i, piece, 2])

    def core_send(rx):
        for i, buf, _ in pre:
            send(buf.at[c_rows(rx, 0)], buf.at[c_rows(rx, 1)], kcs.at[i, rx], kcr.at[i, rx], other)

    def core_wait(rx):
        for i, buf, _ in pre:
            landed(buf.at[c_rows(rx, 1)], kcs.at[i, rx], kcr.at[i, rx])

    def g_forward(c):
        g_wait(2, c)
        g_send(3, c)
        g_wait(1, c)
        g_send(4, c)
        g_send(5, c)

    def g_last(c):
        g_wait(3, c)
        g_send(6, c)

    doc_forward(0)

    landed(kbuf.at[z_rows(3)], kzs.at[0, 0], kzr.at[0, 0])
    send(kbuf.at[z_rows(3)], kbuf.at[z_rows(2)], kzs.at[0, 2], kzr.at[0, 2], zdev[1])
    landed(vbuf.at[z_rows(1)], kzs.at[1, 1], kzr.at[1, 1])
    send(vbuf.at[z_rows(1)], vbuf.at[z_rows(2)], kzs.at[1, 2], kzr.at[1, 2], zdev[3])
    landed(kbuf.at[z_rows(1)], kzs.at[0, 1], kzr.at[0, 1])
    landed(vbuf.at[z_rows(3)], kzs.at[1, 0], kzr.at[1, 0])
    for c in range(1, NC):
        g_send(2, c)
    x_pass(0)
    doc_forward(1)
    for i, buf, _ in pre:
        landed(buf.at[z_rows(2)], kzs.at[i, 2], kzr.at[i, 2])
        send(buf.at[x_rows(0, 1)], buf.at[x_rows(3, 1)], kxs.at[i, 1, 0], kxr.at[i, 1, 0], xdev[1])
        send(buf.at[x_rows(0, 1)], buf.at[x_rows(1, 1)], kxs.at[i, 1, 1], kxr.at[i, 1, 1], xdev[-1])
    for c in local[3:5]:
        c.wait()
    core_send(0)
    g_forward(0)
    core_wait(0)
    pre_forward(0)
    g_forward(1)
    x_pass(1)
    x_rest(0)
    x_rest(1)
    core_send(3)
    core_send(1)
    g_forward(2)
    g_last(0)
    core_wait(3)
    pre_forward(3)
    x_across(0)
    x_across(1)
    core_send(2)
    g_forward(3)
    core_wait(1)
    pre_forward(1)
    g_last(1)
    core_wait(2)
    pre_forward(2)
    g_last(2)

    for hk in range(2):
        lanes = slice(hk * HD, (hk + 1) * HD)
        ot[hk] = dot(vbuf[:, lanes], ebuf[hk], ((0,), (0,))) + dot(vd[:, lanes], edoc[hk], ((0,), (0,)))

    def w_window(ry, rl):
        yy = lax.rem(y + ry % 4, 4)
        src = (zl + rl - 2 * zl * rl) * 4 + yy
        first = (src // 2) * 9 + 4 * lax.rem(src, 2)
        return wraw[:, pl.ds(pl.multiple_of(first * HD, HD), WIN)]

    def project(where, even, odd, waited):
        for c in range(NC):
            if not waited[c % 2]:
                g_wait(odd if c % 2 else even, c)
        hgt[...] += dot(w_window(*where), gbuf[slot_of(*where)])

    for c in local[5:]:
        c.wait()
    hgt[...] = dot(w_window(0, 0), gbuf[0])
    project((1, 0), 1, 0, (True, False))
    project((3, 0), 0, 1, (False, True))
    project((0, 1), 2, 2, (True, True))
    g_last(3)
    project((2, 0), 4, 4, (False, False))
    project((1, 1), 5, 3, (False, True))
    project((3, 1), 3, 5, (True, False))
    project((2, 1), 6, 6, (False, False))

    for hd in range(4):
        hk, cols = hd // 2, slice((hd % 2) * TOK, (hd % 2 + 1) * TOK)
        g = hgt[hd * HD : (hd + 1) * HD, :].astype(BF16).astype(F32)
        inv = 1.0 / jnp.sum(lsum[hk, :, cols], axis=0, keepdims=True)
        scaled = (g * inv).astype(BF16)
        drow[hk, :, cols] = jnp.sum(g * ot[hk, :, cols], axis=0, keepdims=True) * (inv * inv)
        dot_t[hk, :, cols] = scaled
        dos[hk, cols, :] = scaled.T

    def dv_quarter(rx):
        for hk in range(2):
            dv = dot(ebuf[hk, rx * QR : (rx + 1) * QR, :], dos[hk])
            pb[0, rx, :, :, hk * HD : (hk + 1) * HD] = dv.astype(BF16).reshape(2, 256, HD)

    def logit_grads(vv, hk, buf, rows):
        for n in range(2):
            cols = slice(n * TOK, (n + 1) * TOK)
            dp = dot(vv, dot_t[hk, :, cols]) - drow[hk, :, cols]
            buf[hk, rows, cols] = (buf[hk, rows, cols].astype(F32) * dp).astype(BF16)

    def dk_quarter(rx):
        rows = slice(rx * QR, (rx + 1) * QR)
        for hk in range(2):
            lanes = slice(hk * HD, (hk + 1) * HD)
            logit_grads(vbuf[rows, lanes], hk, sbuf, rows)
            dk = dot(sbuf[hk, rows, :], qs[hk]) * SCALE
            pb[1, rx, :, :, lanes] = dk.astype(BF16).reshape(2, 256, HD)

    def pair_send(a, rx):
        send(pb.at[a, rx, 1], pr.at[a, rx], ps.at[a, rx], prs.at[a, rx], other)

    def pair_sum(a, rx):
        landed(pr.at[a, rx], ps.at[a, rx], prs.at[a, rx])
        return pb[a, rx, 0].astype(F32) + pr[a, rx].astype(F32)

    def x_far(a):
        xs[a, 2] = pair_sum(a, 2).astype(BF16)
        send(xs.at[a, 2, 0:128], xc.at[a, 0], xss.at[a, 0], xrs.at[a, 0], xdev[1])
        send(xs.at[a, 2, 128:256], xc.at[a, 1], xss.at[a, 1], xrs.at[a, 1], xdev[-1])

    def x_near(a, n):
        s = pair_sum(a, 1 + 2 * n)
        landed(xc.at[a, n], xss.at[a, n], xrs.at[a, n])
        half = slice(n * 128, (n + 1) * 128)
        rest = slice((1 - n) * 128, (2 - n) * 128)
        xs[a, n, half] = (s[half] + xc[a, n].astype(F32)).astype(BF16)
        xs[a, n, rest] = s[rest].astype(BF16)
        send(xs.at[a, n], xr.at[a, n], xss.at[a, 2 + n], xrs.at[a, 2 + n], xdev[1 - 2 * n])

    def x_total(a):
        t = pair_sum(a, 0)
        for n in range(2):
            landed(xr.at[a, n], xss.at[a, 2 + n], xrs.at[a, 2 + n])
            t = t + xr[a, n].astype(F32)
        tacc[a] = t[0:64]
        zs[a] = t[64:256].astype(BF16)
        for rz in (2, 1, 3):
            piece = slice((rz - 1) * 64, rz * 64)
            send(zs.at[a, piece], zr.at[a, rz - 1], zss.at[a, rz - 1], zrs.at[a, rz - 1], zdev[rz])

    outs = []

    def put(src, dst, n):
        c = pltpu.make_async_copy(src, dst, osem.at[n])
        c.start()
        outs.append(c)

    def z_total(a):
        t = tacc[a]
        for n in range(3):
            landed(zr.at[a, n], zss.at[a, n], zrs.at[a, n])
            t = t + zr[a, n].astype(F32)
        out, dst = ((opv, pdv_hbm), (opk, pdk_hbm))[a]
        out[...] = t.astype(BF16)
        put(out, dst, a)

    dv_quarter(2)
    pair_send(0, 2)
    dv_quarter(1)
    pair_send(0, 1)
    x_far(0)
    dv_quarter(3)
    pair_send(0, 3)
    dv_quarter(0)
    pair_send(0, 0)
    dk_quarter(2)
    pair_send(1, 2)
    x_near(0, 0)
    x_near(0, 1)
    dk_quarter(1)
    pair_send(1, 1)
    x_far(1)
    dk_quarter(3)
    pair_send(1, 3)
    dk_quarter(0)
    pair_send(1, 0)
    x_near(1, 0)
    x_near(1, 1)
    x_total(0)
    for hk in range(2):
        lanes = slice(hk * HD, (hk + 1) * HD)
        logit_grads(vd[:, lanes], hk, sdoc, slice(None))
        odk[:, lanes] = (dot(sdoc[hk], qs[hk]) * SCALE).astype(BF16)
        odv[:, lanes] = dot(edoc[hk], dos[hk]).astype(BF16)
    put(odk, dk_hbm, 2)
    put(odv, dv_hbm, 3)
    x_total(1)

    for hk in range(2):
        lanes = slice(hk * HD, (hk + 1) * HD)
        t = dot(kbuf[:, lanes], sbuf[hk], ((0,), (0,))) + dot(kd[:, lanes], sdoc[hk], ((0,), (0,)))
        for g in range(2):
            hd = hk * 2 + g
            odq[:, hd * HD : (hd + 1) * HD] = (t[:, g * TOK : (g + 1) * TOK] * SCALE).astype(BF16).T
    put(odq, dq_hbm, 4)
    z_total(0)
    z_total(1)
    for c in started:
        c.wait_send()
    for c in outs:
        c.wait()


def finish(*refs):
    for a, b in zip(refs[:5], refs[5:]):
        b[...] = a[...]


def on_device(queries, keys, values, prefix_keys, prefix_values, out_grad, out_weight, doc_lengths):
    sd = jax.ShapeDtypeStruct
    hbm = pl.BlockSpec(memory_space=pl.ANY)
    vm = pltpu.VMEM
    dma = pltpu.SemaphoreType.DMA
    shapes = (
        sd((TOK, 512), BF16),
        sd((TOK, 256), BF16),
        sd((TOK, 256), BF16),
        sd((64, 256), BF16),
        sd((64, 256), BF16),
    )
    grads = pl.pallas_call(
        kernel,
        out_shape=shapes,
        in_specs=[pl.BlockSpec(memory_space=pltpu.SMEM)] + [hbm] * 7,
        out_specs=(hbm,) * 5,
        scratch_shapes=[
            vm((TOK, 512), BF16),
            vm((TOK, 256), BF16),
            vm((TOK, 256), BF16),
            vm((8, WIN, TOK), BF16),
            vm((512, 4608), BF16),
            vm((PRE, 256), BF16),
            vm((PRE, 256), BF16),
            vm((2, PRE, QW), BF16),
            vm((2, PRE, QW), BF16),
            vm((2, TOK, QW), BF16),
            vm((2, TOK, QW), BF16),
            vm((2, HD, QW), BF16),
            vm((2, QW, HD), BF16),
            vm((2, HD, QW), BF16),
            vm((2, QW, HD), BF16),
            vm((2, HD, QW), F32),
            vm((2, 8, QW), F32),
            vm((2, 1, QW), F32),
            vm((512, TOK), F32),
            vm((2, 4, 2, 256, 256), BF16),
            vm((2, 4, 256, 256), BF16),
            vm((2, 3, 256, 256), BF16),
            vm((2, 2, 128, 256), BF16),
            vm((2, 2, 256, 256), BF16),
            vm((2, 64, 256), F32),
            vm((2, 192, 256), BF16),
            vm((2, 3, 64, 256), BF16),
            vm((TOK, 512), BF16),
            vm((TOK, 256), BF16),
            vm((TOK, 256), BF16),
            vm((64, 256), BF16),
            vm((64, 256), BF16),
            dma((7,)),
            dma((7, NC)),
            dma((7, NC)),
            dma((2, 3)),
            dma((2, 3)),
            dma((2, 2, 3)),
            dma((2, 2, 3)),
            dma((2, 4)),
            dma((2, 4)),
            dma((2, 4)),
            dma((2, 4)),
            dma((2, 4)),
            dma((2, 4)),
            dma((2, 3)),
            dma((2, 3)),
            dma((5,)),
        ],
        compiler_params=pltpu.CompilerParams(
            collective_id=0, has_side_effects=True, vmem_limit_bytes=60 * 1024 * 1024
        ),
    )(doc_lengths, queries, keys, values, prefix_keys, prefix_values, out_grad.T, out_weight)
    return pl.pallas_call(
        finish,
        out_shape=shapes,
        in_specs=[pl.BlockSpec(memory_space=vm)] * 5,
        out_specs=(pl.BlockSpec(memory_space=vm),) * 5,
    )(*grads)


def solution(mesh):
    return jax.shard_map(
        on_device,
        mesh=mesh,
        in_specs=(P("docs", "heads"),) * 6 + (P("heads", None), P("docs", None)),
        out_specs=(P("docs", "heads"),) * 5,
        check_vma=False,
    )
```

```python
import jax
import jax.numpy as jnp
from jax import lax
from jax.experimental import pallas as pl
from jax.experimental.pallas import tpu as pltpu
from jax.sharding import PartitionSpec as P

HD = 128
SOFTCAP = 50.0
SCALE = 1.0 / 12.0
LOG2E = 1.4426950408889634
F32 = jnp.float32
BF16 = jnp.bfloat16
MESH = pl.DeviceIdType.MESH

TOK = 512
FEAT = 576
LAY = 4 * FEAT
NC = 4
CH = TOK // NC
QW = 1024
PRE = 2048
QR = 512


def dot(a, b, dims=((1,), (0,))):
    return lax.dot_general(a, b, (dims, ((), ())), preferred_element_type=F32)


def kernel(
    len_ref, q_hbm, k_hbm, v_hbm, pk_hbm, pv_hbm, og_hbm, w_hbm,
    dq_hbm, dk_hbm, dv_hbm, pdk_hbm, pdv_hbm,
    qb, kd, vd, gl, wl, wp, hs, hr, kbuf, vbuf, ebuf, sbuf, edoc, sdoc, qt, qs, dot_t, dos, ot, lsum, drow, hgt,
    pb, pr, xs, xr, tacc, zs, zr, odq, odk, odv, opk, opv,
    ls, gs, gr, hss, hrs, wzs, wzr, wxs, wxr, wcs, wcr, kzs, kzr, kxs, kxr, kcs, kcr, ps, prs, xss, xrs, zss, zrs, osem,
):
    d = lax.axis_index("docs")
    h = lax.axis_index("heads")
    core = lax.rem(d, 2)
    x = lax.rem(d // 2, 4)
    zh = d // 8
    zl = h // 4
    y = lax.rem(h, 4)

    def doc_id(zz, xx, cc):
        return {"docs": (lax.rem(zz + 4, 4) * 4 + lax.rem(xx + 4, 4)) * 2 + cc}

    def head_id(zz, yy):
        return {"heads": zz * 4 + lax.rem(yy + 4, 4)}

    other = doc_id(zh, x, 1 - core)
    xdev = {1: doc_id(zh, x + 1, core), -1: doc_id(zh, x - 1, core), -2: doc_id(zh, x - 2, core)}
    xdev[-3] = xdev[1]
    zdev = {1: doc_id(zh + 1, x, core), 2: doc_id(zh + 2, x, core), 3: doc_id(zh + 3, x, core)}
    ydev = {1: head_id(zl, y + 1), -1: head_id(zl, y - 1)}
    pdev = head_id(1 - zl, y)
    zz = lax.rem(zh + 2 * zl + 3, 4)
    wdev = {"docs": (zz * 4 + x) * 2 + core, "heads": (1 - zl) * 4 + y}

    barrier = pltpu.get_barrier_semaphore()
    peers = (other, xdev[1], xdev[-1], xdev[-2], zdev[1], zdev[2], zdev[3], ydev[1], ydev[-1], pdev, wdev)
    for p in peers:
        pl.semaphore_signal(barrier, inc=1, device_id=p, device_id_type=MESH)

    def g_rows(ry):
        return pl.ds(pl.multiple_of(lax.rem(y + ry + 4, 4) * FEAT, FEAT), FEAT)

    def layer(zz):
        return pl.ds(pl.multiple_of(zz * LAY, LAY), LAY)

    local = [
        pltpu.make_async_copy(q_hbm, qb, ls.at[0]),
        pltpu.make_async_copy(k_hbm, kd, ls.at[1]),
        pltpu.make_async_copy(v_hbm, vd, ls.at[2]),
        pltpu.make_async_copy(pk_hbm, kbuf.at[0, 0, 0], ls.at[3]),
        pltpu.make_async_copy(pv_hbm, vbuf.at[0, 0, 0], ls.at[4]),
        pltpu.make_async_copy(og_hbm, gl.at[g_rows(0)], ls.at[5]),
        pltpu.make_async_copy(w_hbm.at[:, layer(zl)], wl, ls.at[6]),
    ]
    for c in local:
        c.start()
    pl.semaphore_wait(barrier, len(peers))

    started = []

    def remote(src, dst, ssem, rsem, device):
        return pltpu.make_async_remote_copy(
            src_ref=src, dst_ref=dst, send_sem=ssem, recv_sem=rsem, device_id=device, device_id_type=MESH
        )

    def send(*args):
        c = remote(*args)
        c.start()
        started.append(c)

    def landed(dst, ssem, rsem):
        remote(dst, dst, ssem, rsem, other).wait_recv()

    def g_route(kind, c):
        s = 1 if c % 2 == 0 else -1
        return ((0, ydev[s], -s), (0, ydev[-s], s), (s, ydev[-s], 2))[kind]

    def g_send(kind, c):
        ry, to, _ = g_route(kind, c)
        cols = pl.ds(c * CH, CH)
        at = gl.at[g_rows(ry), cols]
        send(og_hbm.at[:, cols] if kind < 2 else at, at, gs.at[kind, c], gr.at[kind, c], to)

    def g_wait(kind, c):
        landed(gl.at[g_rows(g_route(kind, c)[2]), pl.ds(c * CH, CH)], gs.at[kind, c], gr.at[kind, c])

    def g_forward(c):
        g_wait(1, c)
        g_send(2, c)

    def w_rows(odd, rc, part):
        first = lax.rem(x + odd, 2) * 256 + (core if rc == 0 else 1 - core) * 128
        if part is None:
            return pl.ds(pl.multiple_of(first, 128), 128)
        return pl.ds(pl.multiple_of(first + part * 64, 64), 64)

    def w_send():
        for part, to in ((0, pdev), (1, wdev)):
            rows = w_rows(0, 0, part)
            send(w_hbm.at[rows, layer(1 - zl)], wp.at[rows], wzs.at[part], wzr.at[part], to)

    def w_spread(part):
        rows = w_rows(0, 0, part)
        landed(wp.at[rows], wzs.at[part], wzr.at[part])
        send(wp.at[rows], wp.at[rows], wxs.at[part], wxr.at[part], xdev[1 - 2 * part])

    def w_core(odd):
        rows = w_rows(odd, 0, None)
        send(wp.at[rows], wp.at[rows], wcs.at[odd], wcr.at[odd], other)

    def w_across():
        for part in range(2):
            landed(wp.at[w_rows(1, 0, part)], wxs.at[part], wxr.at[part])
        w_core(1)

    def w_wait(odd):
        landed(wp.at[w_rows(odd, 1, None)], wcs.at[odd], wcr.at[odd])

    pre = ((0, kbuf, pk_hbm), (1, vbuf, pv_hbm))
    for i, buf, src in pre:
        send(src, buf.at[0, 0, 3], kzs.at[i, 2], kzr.at[i, 2], zdev[1])
        send(src, buf.at[0, 0, 1], kzs.at[i, 0], kzr.at[i, 0], zdev[3])
    w_send()
    for i, buf, src in pre:
        send(src, buf.at[0, 0, 2], kzs.at[i, 1], kzr.at[i, 1], zdev[2])
    for i, buf, src in pre:
        for rx in (1, 3, 2):
            send(src, buf.at[rx, 0, 0], kxs.at[i, 0, rx - 1], kxr.at[i, 0, rx - 1], xdev[-rx])
    for c in range(NC):
        g_send(0, c)
        g_send(1, c)
    for c in local[:3]:
        c.wait()
    for hd in range(4):
        blk = qb[:, hd * HD : (hd + 1) * HD]
        qs[hd // 2, (hd % 2) * TOK : (hd % 2 + 1) * TOK, :] = blk
        qt[hd // 2, :, (hd % 2) * TOK : (hd % 2 + 1) * TOK] = blk.T

    b0 = len_ref[0, 0]
    b1 = b0 + len_ref[0, 1]
    b2 = b1 + len_ref[0, 2]

    def segment(p):
        return (p >= b0).astype(jnp.int32) + (p >= b1).astype(jnp.int32) + (p >= b2).astype(jnp.int32)

    def weights(kk, hk, cols, mask):
        t = jnp.tanh(dot(kk, qt[hk, :, cols]) * (SCALE / SOFTCAP))
        e = jnp.exp2(t * (SOFTCAP * LOG2E))
        if mask is not None:
            e = jnp.where(mask, e, 0.0)
        return e, e * (1.0 - t * t)

    def partial_sums(e):
        return jnp.sum(e.reshape(e.shape[0] // 8, 8, e.shape[1]), axis=0)

    def doc_forward(hk):
        lsum[hk] = jnp.zeros((8, QW), F32)
        for j in range(4):
            rows = slice(j * HD, (j + 1) * HD)
            lo, hi = j * HD, min(TOK, (j + 3) * HD)
            key = lo + lax.broadcasted_iota(jnp.int32, (HD, hi - lo), 0)
            row = lo + lax.broadcasted_iota(jnp.int32, (HD, hi - lo), 1)
            mask = (key <= row) & (segment(key) == segment(row))
            for g in range(2):
                cols = slice(g * TOK + lo, g * TOK + hi)
                e, s = weights(kd[rows, hk * HD : (hk + 1) * HD], hk, cols, mask)
                lsum[hk, :, cols] += partial_sums(e)
                edoc[hk, rows, cols] = e.astype(BF16)
                sdoc[hk, rows, cols] = s.astype(BF16)
                for a, b in ((0, lo), (hi, TOK)):
                    if a < b:
                        edoc[hk, rows, g * TOK + a : g * TOK + b] = jnp.zeros((HD, b - a), BF16)
                        sdoc[hk, rows, g * TOK + a : g * TOK + b] = jnp.zeros((HD, b - a), BF16)

    def pre_forward(rz):
        def one(hk, carry):
            lanes = pl.ds(pl.multiple_of(hk * HD, HD), HD)
            e, s = weights(kbuf[:, :, rz, :, lanes].reshape(QR, HD), hk, slice(None), None)
            lsum[hk] += partial_sums(e)
            ebuf[hk, :, :, rz] = e.astype(BF16).reshape(4, 2, 64, QW)
            sbuf[hk, :, :, rz] = s.astype(BF16).reshape(4, 2, 64, QW)
            return carry

        lax.fori_loop(0, 2, one, 0)

    def z_landed(rz):
        for i, buf, _ in pre:
            landed(buf.at[0, 0, rz], kzs.at[i, rz - 1], kzr.at[i, rz - 1])

    def x_near(rz):
        for i, buf, _ in pre:
            for rx in (1, 3):
                send(buf.at[0, 0, rz], buf.at[rx, 0, rz], kxs.at[i, rz, rx - 1], kxr.at[i, rz, rx - 1], xdev[-rx])

    def x_landed(i, rx, rz):
        landed(pre[i][1].at[rx, 0, rz], kxs.at[i, rz, rx - 1], kxr.at[i, rz, rx - 1])

    def x_pass(rz):
        for i, got, to in ((0, 3, 1), (1, 1, -1)):
            x_landed(i, got, rz)
            buf = pre[i][1]
            send(buf.at[got, 0, rz], buf.at[2, 0, rz], kxs.at[i, rz, 1], kxr.at[i, rz, 1], xdev[to])

    def core_send(rz):
        for i, buf, _ in pre:
            for rx in (1, 3, 2):
                if rz == 0 or rx == 2 or rx == (1, 3)[i]:
                    x_landed(i, rx, rz)
            send(buf.at[:, 0, rz], buf.at[:, 1, rz], kcs.at[i, rz], kcr.at[i, rz], other)

    def core_wait(rz):
        for i, buf, _ in pre:
            landed(buf.at[:, 1, rz], kcs.at[i, rz], kcr.at[i, rz])

    doc_forward(0)
    doc_forward(1)

    def project(w, n):
        return dot(w, gl[:, n * 256 : (n + 1) * 256])

    def g_last(n):
        for c in (2 * n, 2 * n + 1):
            g_wait(0, c)
            g_wait(2, c)

    def own(n):
        hgt[:, n * 256 : (n + 1) * 256] = project(wl[...], n)

    def partner(n, odd):
        rows = pl.ds(pl.multiple_of(lax.rem(x + odd, 2) * 256, 256), 256)
        cols = pl.ds(n * 256, 256)
        hs[rows, cols] = project(wp[rows, :], n).astype(BF16)
        send(hs.at[rows, cols], hr.at[rows, cols], hss.at[n, odd], hrs.at[n, odd], pdev)

    g_forward(0)
    for c in local[3:5]:
        c.wait()
    core_send(0)
    for rz in (1, 3):
        z_landed(rz)
        x_near(rz)
    g_forward(1)
    core_wait(0)
    pre_forward(0)
    x_pass(1)
    g_forward(2)
    w_spread(0)
    w_spread(1)
    w_core(0)
    x_pass(3)
    core_send(1)
    g_forward(3)
    core_wait(1)
    pre_forward(1)
    z_landed(2)
    x_near(2)
    g_last(0)
    for c in local[5:]:
        c.wait()
    w_wait(0)
    partner(0, 0)
    own(0)
    g_last(1)
    partner(1, 0)
    w_across()
    core_send(3)
    x_pass(2)
    w_wait(1)
    partner(0, 1)
    partner(1, 1)
    own(1)
    core_send(2)
    core_wait(3)
    pre_forward(3)
    core_wait(2)
    pre_forward(2)
    for hk in range(2):
        lanes = slice(hk * HD, (hk + 1) * HD)
        vv = vbuf[:, :, :, :, lanes].reshape(PRE, HD)
        ot[hk] = dot(vv, ebuf[hk].reshape(PRE, QW), ((0,), (0,))) + dot(vd[:, lanes], edoc[hk], ((0,), (0,)))
    for n in range(2):
        cols = pl.ds(n * 256, 256)
        for odd in range(2):
            rows = pl.ds(pl.multiple_of(lax.rem(x + odd, 2) * 256, 256), 256)
            landed(hr.at[rows, cols], hss.at[n, odd], hrs.at[n, odd])
        hgt[:, cols] += hr[:, cols].astype(F32)

    for hd in range(4):
        hk, cols = hd // 2, slice((hd % 2) * TOK, (hd % 2 + 1) * TOK)
        g = hgt[hd * HD : (hd + 1) * HD, :].astype(BF16).astype(F32)
        inv = 1.0 / jnp.sum(lsum[hk, :, cols], axis=0, keepdims=True)
        scaled = (g * inv).astype(BF16)
        drow[hk, :, cols] = jnp.sum(g * ot[hk, :, cols], axis=0, keepdims=True) * (inv * inv)
        dot_t[hk, :, cols] = scaled
        dos[hk, cols, :] = scaled.T

    def put_terms(a, hk, rz, t):
        t = t.astype(BF16).reshape(4, 2, 64, HD)
        for rc in range(2):
            pb[rz, a, rc, :, :, hk * HD : (hk + 1) * HD] = t[:, rc]

    def dv_block(rz):
        for hk in range(2):
            put_terms(0, hk, rz, dot(ebuf[hk, :, :, rz].reshape(QR, QW), dos[hk]))
        pair_send(rz, 0)

    def logit_grads(vv, hk, s, cols):
        dp = dot(vv, dot_t[hk, :, cols]) - drow[hk, :, cols]
        return (s.astype(F32) * dp).astype(BF16)

    def dk_block(rz):
        for hk in range(2):
            vv = vbuf[:, :, rz, :, hk * HD : (hk + 1) * HD].reshape(QR, HD)
            for n in range(2):
                cols = slice(n * TOK, (n + 1) * TOK)
                ds = logit_grads(vv, hk, sbuf[hk, :, :, rz, :, cols].reshape(QR, TOK), cols)
                sbuf[hk, :, :, rz, :, cols] = ds.reshape(4, 2, 64, TOK)
            put_terms(1, hk, rz, dot(sbuf[hk, :, :, rz].reshape(QR, QW), qs[hk]) * SCALE)
        pair_send(rz, 1)

    def pair_send(rz, a):
        send(pb.at[rz, a, 1], pr.at[rz, a], ps.at[rz, a], prs.at[rz, a], other)

    def pair_sum(rz, a, rx):
        return pb[rz, a, 0, rx].astype(F32) + pr[rz, a, rx].astype(F32)

    def x_send(rz, a):
        landed(pr.at[rz, a], ps.at[rz, a], prs.at[rz, a])
        for rx in (2, 1, 3):
            n = rx - 1
            xs[rz, a, n] = pair_sum(rz, a, rx).astype(BF16)
            send(xs.at[rz, a, n], xr.at[rz, a, n], xss.at[rz, a, n], xrs.at[rz, a, n], xdev[rx - 4])

    def x_total(rz):
        for a in range(2):
            t = pair_sum(rz, a, 0)
            for n in range(3):
                landed(xr.at[rz, a, n], xss.at[rz, a, n], xrs.at[rz, a, n])
                t = t + xr[rz, a, n].astype(F32)
            if rz:
                zs[rz - 1, a] = t.astype(BF16)
            else:
                tacc[a] = t
        if rz:
            send(zs.at[rz - 1], zr.at[rz - 1], zss.at[rz - 1], zrs.at[rz - 1], zdev[rz])

    outs = []

    def put(src, dst, n):
        c = pltpu.make_async_copy(src, dst, osem.at[n])
        c.start()
        outs.append(c)

    def z_in(n):
        landed(zr.at[n], zss.at[n], zrs.at[n])

    dv_block(2)
    dk_block(2)
    x_send(2, 0)
    dv_block(1)
    x_send(2, 1)
    dk_block(1)
    x_send(1, 0)
    dv_block(3)
    x_send(1, 1)
    dk_block(3)
    x_send(3, 0)
    dv_block(0)
    x_send(3, 1)
    dk_block(0)
    x_send(0, 0)
    x_total(2)

    def doc_backward(hk):
        lanes = slice(hk * HD, (hk + 1) * HD)
        for n in range(2):
            cols = slice(n * TOK, (n + 1) * TOK)
            sdoc[hk, :, cols] = logit_grads(vd[:, lanes], hk, sdoc[hk, :, cols], cols)
        odk[:, lanes] = (dot(sdoc[hk], qs[hk]) * SCALE).astype(BF16)
        odv[:, lanes] = dot(edoc[hk], dos[hk]).astype(BF16)

    doc_backward(0)
    x_send(0, 1)
    x_total(1)
    doc_backward(1)
    put(odk, dk_hbm, 2)
    put(odv, dv_hbm, 3)
    x_total(3)
    for hk in range(2):
        lanes = slice(hk * HD, (hk + 1) * HD)
        kk = kbuf[:, :, :, :, lanes].reshape(PRE, HD)
        t = dot(kk, sbuf[hk].reshape(PRE, QW), ((0,), (0,))) + dot(kd[:, lanes], sdoc[hk], ((0,), (0,)))
        for g in range(2):
            hd = hk * 2 + g
            odq[:, hd * HD : (hd + 1) * HD] = (t[:, g * TOK : (g + 1) * TOK] * SCALE).astype(BF16).T
    put(odq, dq_hbm, 4)
    x_total(0)
    for n in (1, 0, 2):
        z_in(n)
    for a, out, dst in ((0, opv, pdv_hbm), (1, opk, pdk_hbm)):
        out[...] = (tacc[a] + zr[0, a].astype(F32) + zr[1, a].astype(F32) + zr[2, a].astype(F32)).astype(BF16)
        put(out, dst, a)
    for c in started:
        c.wait_send()
    for c in outs:
        c.wait()


def finish(*refs):
    ins, outs, held, sem = refs[:5], refs[5:10], refs[10:15], refs[15]
    into = [pltpu.make_async_copy(a, b, sem.at[0, i]) for i, (a, b) in enumerate(zip(ins, held))]
    back = [pltpu.make_async_copy(a, b, sem.at[1, i]) for i, (a, b) in enumerate(zip(held, outs))]
    for c in into:
        c.start()
    for a, b in zip(into, back):
        a.wait()
        b.start()
    for c in back:
        c.wait()


def on_device(queries, keys, values, prefix_keys, prefix_values, out_grad, out_weight, doc_lengths):
    sd = jax.ShapeDtypeStruct
    hbm = pl.BlockSpec(memory_space=pl.ANY)
    vm = pltpu.VMEM
    dma = pltpu.SemaphoreType.DMA
    shapes = (
        sd((TOK, 512), BF16),
        sd((TOK, 256), BF16),
        sd((TOK, 256), BF16),
        sd((64, 256), BF16),
        sd((64, 256), BF16),
    )
    grads = pl.pallas_call(
        kernel,
        out_shape=shapes,
        in_specs=[pl.BlockSpec(memory_space=pltpu.SMEM)] + [hbm] * 7,
        out_specs=(hbm,) * 5,
        scratch_shapes=[
            vm((TOK, 512), BF16),
            vm((TOK, 256), BF16),
            vm((TOK, 256), BF16),
            vm((LAY, TOK), BF16),
            vm((512, LAY), BF16),
            vm((512, LAY), BF16),
            vm((512, TOK), BF16),
            vm((512, TOK), BF16),
            vm((4, 2, 4, 64, 256), BF16),
            vm((4, 2, 4, 64, 256), BF16),
            vm((2, 4, 2, 4, 64, QW), BF16),
            vm((2, 4, 2, 4, 64, QW), BF16),
            vm((2, TOK, QW), BF16),
            vm((2, TOK, QW), BF16),
            vm((2, HD, QW), BF16),
            vm((2, QW, HD), BF16),
            vm((2, HD, QW), BF16),
            vm((2, QW, HD), BF16),
            vm((2, HD, QW), F32),
            vm((2, 8, QW), F32),
            vm((2, 1, QW), F32),
            vm((512, TOK), F32),
            vm((4, 2, 2, 4, 64, 256), BF16),
            vm((4, 2, 4, 64, 256), BF16),
            vm((4, 2, 3, 64, 256), BF16),
            vm((4, 2, 3, 64, 256), BF16),
            vm((2, 64, 256), F32),
            vm((3, 2, 64, 256), BF16),
            vm((3, 2, 64, 256), BF16),
            vm((TOK, 512), BF16),
            vm((TOK, 256), BF16),
            vm((TOK, 256), BF16),
            vm((64, 256), BF16),
            vm((64, 256), BF16),
            dma((7,)),
            dma((3, NC)),
            dma((3, NC)),
            dma((2, 2)),
            dma((2, 2)),
            dma((2,)),
            dma((2,)),
            dma((2,)),
            dma((2,)),
            dma((2,)),
            dma((2,)),
            dma((2, 3)),
            dma((2, 3)),
            dma((2, 4, 3)),
            dma((2, 4, 3)),
            dma((2, 4)),
            dma((2, 4)),
            dma((4, 2)),
            dma((4, 2)),
            dma((4, 2, 3)),
            dma((4, 2, 3)),
            dma((3,)),
            dma((3,)),
            dma((5,)),
        ],
        compiler_params=pltpu.CompilerParams(
            collective_id=0, has_side_effects=True, vmem_limit_bytes=60 * 1024 * 1024
        ),
    )(doc_lengths, queries, keys, values, prefix_keys, prefix_values, out_grad.T, out_weight)
    return pl.pallas_call(
        finish,
        out_shape=shapes,
        in_specs=[hbm] * 5,
        out_specs=(hbm,) * 5,
        scratch_shapes=[vm(s.shape, s.dtype) for s in shapes] + [dma((2, 5))],
    )(*grads)


def solution(mesh):
    return jax.shard_map(
        on_device,
        mesh=mesh,
        in_specs=(P("docs", "heads"),) * 6 + (P("heads", None), P("docs", None)),
        out_specs=(P("docs", "heads"),) * 5,
        check_vma=False,
    )
```

```python
import jax
import jax.numpy as jnp
from jax import lax
from jax.experimental import pallas as pl
from jax.experimental.pallas import tpu as pltpu
from jax.sharding import PartitionSpec as P

HD = 128
SOFTCAP = 50.0
SCALE = 1.0 / 12.0
LOG2E = 1.4426950408889634
F32 = jnp.float32
BF16 = jnp.bfloat16
MESH = pl.DeviceIdType.MESH

TOK = 512
FEAT = 576
LAY = 4 * FEAT
NC = 4
CH = TOK // NC
QW = 1024
PRE = 2048
QR = 512


def dot(a, b, dims=((1,), (0,))):
    return lax.dot_general(a, b, (dims, ((), ())), preferred_element_type=F32)


def kernel(
    len_ref, q_hbm, k_hbm, v_hbm, pk_hbm, pv_hbm, og_hbm, w_hbm,
    dq_hbm, dk_hbm, dv_hbm, pdk_hbm, pdv_hbm,
    qb, kd, vd, gl, wl, wp, hs, hr, kbuf, vbuf, ebuf, sbuf, edoc, sdoc, qt, qs, dot_t, dos, ot, lsum, drow, hgt,
    pb, pr, vs, vr, xs, xr, tacc, zs, zr, odq, odk, odv, opk, opv,
    ls, gs, gr, hss, hrs, wzs, wzr, wcs, wcr, kzs, kzr, kxs, kxr, kcs, kcr, ps, prs, vss, vrs, xss, xrs, zss, zrs, osem,
):
    d = lax.axis_index("docs")
    h = lax.axis_index("heads")
    core = lax.rem(d, 2)
    x = lax.rem(d // 2, 4)
    zh = d // 8
    zl = h // 4
    y = lax.rem(h, 4)

    def doc_id(zz, xx, cc):
        return {"docs": (lax.rem(zz + 4, 4) * 4 + lax.rem(xx + 4, 4)) * 2 + cc}

    def head_id(zz, yy):
        return {"heads": zz * 4 + lax.rem(yy + 4, 4)}

    other = doc_id(zh, x, 1 - core)
    xdev = {1: doc_id(zh, x + 1, core), -1: doc_id(zh, x - 1, core), -2: doc_id(zh, x - 2, core)}
    xdev[-3] = xdev[1]
    zdev = {1: doc_id(zh + 1, x, core), 2: doc_id(zh + 2, x, core), 3: doc_id(zh + 3, x, core)}
    ydev = {1: head_id(zl, y + 1), -1: head_id(zl, y - 1)}
    pdev = head_id(1 - zl, y)
    zz = lax.rem(zh + 2 * zl + 3, 4)
    wdev = {"docs": (zz * 4 + x) * 2 + core, "heads": (1 - zl) * 4 + y}

    barrier = pltpu.get_barrier_semaphore()
    peers = (other, xdev[1], xdev[-1], xdev[-2], zdev[1], zdev[2], zdev[3], ydev[1], ydev[-1], pdev, wdev)
    for p in peers:
        pl.semaphore_signal(barrier, inc=1, device_id=p, device_id_type=MESH)

    def g_rows(ry):
        return pl.ds(pl.multiple_of(lax.rem(y + ry + 4, 4) * FEAT, FEAT), FEAT)

    def layer(zz):
        return pl.ds(pl.multiple_of(zz * LAY, LAY), LAY)

    local = [
        pltpu.make_async_copy(q_hbm, qb, ls.at[0]),
        pltpu.make_async_copy(k_hbm, kd, ls.at[1]),
        pltpu.make_async_copy(v_hbm, vd, ls.at[2]),
        pltpu.make_async_copy(pk_hbm, kbuf.at[0, 0, 0], ls.at[3]),
        pltpu.make_async_copy(pv_hbm, vbuf.at[0, 0, 0], ls.at[4]),
        pltpu.make_async_copy(og_hbm, gl.at[g_rows(0)], ls.at[5]),
        pltpu.make_async_copy(w_hbm.at[:, layer(zl)], wl, ls.at[6]),
    ]
    for c in local:
        c.start()
    pl.semaphore_wait(barrier, len(peers))

    started = []

    def remote(src, dst, ssem, rsem, device):
        return pltpu.make_async_remote_copy(
            src_ref=src, dst_ref=dst, send_sem=ssem, recv_sem=rsem, device_id=device, device_id_type=MESH
        )

    def send(*args):
        c = remote(*args)
        c.start()
        started.append(c)

    def landed(dst, ssem, rsem):
        remote(dst, dst, ssem, rsem, other).wait_recv()

    def g_route(kind, c):
        s = 1 if c % 2 == 0 else -1
        return ((0, ydev[s], -s), (0, ydev[-s], s), (s, ydev[-s], 2))[kind]

    def g_send(kind, c):
        ry, to, _ = g_route(kind, c)
        cols = pl.ds(c * CH, CH)
        at = gl.at[g_rows(ry), cols]
        send(og_hbm.at[:, cols] if kind < 2 else at, at, gs.at[kind, c], gr.at[kind, c], to)

    def g_wait(kind, c):
        landed(gl.at[g_rows(g_route(kind, c)[2]), pl.ds(c * CH, CH)], gs.at[kind, c], gr.at[kind, c])

    def g_forward(c):
        g_wait(1, c)
        g_send(2, c)

    def w_rows(stage, rc, part):
        first = stage * 256 + (core if rc == 0 else 1 - core) * 128
        if part is None:
            return pl.ds(pl.multiple_of(first, 128), 128)
        return pl.ds(pl.multiple_of(first + part * 64, 64), 64)

    def w_send(stage):
        for part, to in ((0, pdev), (1, wdev)):
            rows = w_rows(stage, 0, part)
            send(w_hbm.at[rows, layer(1 - zl)], wp.at[rows], wzs.at[stage, part], wzr.at[stage, part], to)

    def w_core(stage):
        for part in range(2):
            landed(wp.at[w_rows(stage, 0, part)], wzs.at[stage, part], wzr.at[stage, part])
        rows = w_rows(stage, 0, None)
        send(wp.at[rows], wp.at[rows], wcs.at[stage], wcr.at[stage], other)

    def w_wait(stage):
        landed(wp.at[w_rows(stage, 1, None)], wcs.at[stage], wcr.at[stage])

    pre = ((0, kbuf, pk_hbm), (1, vbuf, pv_hbm))
    for i, buf, src in pre:
        send(src, buf.at[0, 0, 3], kzs.at[i, 2], kzr.at[i, 2], zdev[1])
        send(src, buf.at[0, 0, 1], kzs.at[i, 0], kzr.at[i, 0], zdev[3])
    w_send(0)
    for i, buf, src in pre:
        send(src, buf.at[0, 0, 2], kzs.at[i, 1], kzr.at[i, 1], zdev[2])
    w_send(1)
    for i, buf, src in pre:
        for rx in (1, 3, 2):
            send(src, buf.at[rx, 0, 0], kxs.at[i, 0, rx - 1], kxr.at[i, 0, rx - 1], xdev[-rx])
    for c in range(3):
        g_send(0, c)
        g_send(1, c)
    for c in local[:3]:
        c.wait()
    for hd in range(4):
        blk = qb[:, hd * HD : (hd + 1) * HD]
        qs[hd // 2, (hd % 2) * TOK : (hd % 2 + 1) * TOK, :] = blk
        qt[hd // 2, :, (hd % 2) * TOK : (hd % 2 + 1) * TOK] = blk.T

    b0 = len_ref[0, 0]
    b1 = b0 + len_ref[0, 1]
    b2 = b1 + len_ref[0, 2]

    def segment(p):
        return (p >= b0).astype(jnp.int32) + (p >= b1).astype(jnp.int32) + (p >= b2).astype(jnp.int32)

    def weights(kk, hk, cols, mask):
        t = jnp.tanh(dot(kk, qt[hk, :, cols]) * (SCALE / SOFTCAP))
        e = jnp.exp2(t * (SOFTCAP * LOG2E))
        if mask is not None:
            e = jnp.where(mask, e, 0.0)
        return e, e * (1.0 - t * t)

    def partial_sums(e):
        return jnp.sum(e.reshape(e.shape[0] // 8, 8, e.shape[1]), axis=0)

    def doc_forward(hk):
        lsum[hk] = jnp.zeros((8, QW), F32)
        for j in range(4):
            rows = slice(j * HD, (j + 1) * HD)
            lo, hi = j * HD, min(TOK, (j + 3) * HD)
            key = lo + lax.broadcasted_iota(jnp.int32, (HD, hi - lo), 0)
            row = lo + lax.broadcasted_iota(jnp.int32, (HD, hi - lo), 1)
            mask = (key <= row) & (segment(key) == segment(row))
            for g in range(2):
                cols = slice(g * TOK + lo, g * TOK + hi)
                e, s = weights(kd[rows, hk * HD : (hk + 1) * HD], hk, cols, mask)
                lsum[hk, :, cols] += partial_sums(e)
                edoc[hk, rows, cols] = e.astype(BF16)
                sdoc[hk, rows, cols] = s.astype(BF16)
                for a, b in ((0, lo), (hi, TOK)):
                    if a < b:
                        edoc[hk, rows, g * TOK + a : g * TOK + b] = jnp.zeros((HD, b - a), BF16)
                        sdoc[hk, rows, g * TOK + a : g * TOK + b] = jnp.zeros((HD, b - a), BF16)

    def pre_forward(rz):
        def one(hk, carry):
            lanes = pl.ds(pl.multiple_of(hk * HD, HD), HD)
            e, s = weights(kbuf[:, :, rz, :, lanes].reshape(QR, HD), hk, slice(None), None)
            lsum[hk] += partial_sums(e)
            ebuf[hk, :, :, rz] = e.astype(BF16).reshape(4, 2, 64, QW)
            sbuf[hk, :, :, rz] = s.astype(BF16).reshape(4, 2, 64, QW)
            return carry

        lax.fori_loop(0, 2, one, 0)

    def z_landed(rz):
        for i, buf, _ in pre:
            landed(buf.at[0, 0, rz], kzs.at[i, rz - 1], kzr.at[i, rz - 1])

    def x_near(rz):
        for i, buf, _ in pre:
            for rx in (1, 3):
                send(buf.at[0, 0, rz], buf.at[rx, 0, rz], kxs.at[i, rz, rx - 1], kxr.at[i, rz, rx - 1], xdev[-rx])

    def x_landed(i, rx, rz):
        landed(pre[i][1].at[rx, 0, rz], kxs.at[i, rz, rx - 1], kxr.at[i, rz, rx - 1])

    def x_pass(rz):
        for i, got, to in ((0, 3, 1), (1, 1, -1)):
            x_landed(i, got, rz)
            buf = pre[i][1]
            send(buf.at[got, 0, rz], buf.at[2, 0, rz], kxs.at[i, rz, 1], kxr.at[i, rz, 1], xdev[to])

    def core_send(rz):
        for i, buf, _ in pre:
            for rx in (1, 3, 2):
                if rz == 0 or rx == 2 or rx == (1, 3)[i]:
                    x_landed(i, rx, rz)
            send(buf.at[:, 0, rz], buf.at[:, 1, rz], kcs.at[i, rz], kcr.at[i, rz], other)

    def core_wait(rz):
        for i, buf, _ in pre:
            landed(buf.at[:, 1, rz], kcs.at[i, rz], kcr.at[i, rz])

    doc_forward(0)
    doc_forward(1)

    def project(w, n):
        return dot(w, gl[:, n * 256 : (n + 1) * 256])

    def g_last(n):
        for c in (2 * n, 2 * n + 1):
            g_wait(0, c)
            g_wait(2, c)

    def own(n):
        hgt[:, n * 256 : (n + 1) * 256] = project(wl[...], n)

    def partner(n, stage):
        rows = pl.ds(stage * 256, 256)
        cols = pl.ds(n * 256, 256)
        hs[rows, cols] = project(wp[rows, :], n).astype(BF16)
        send(hs.at[rows, cols], hr.at[rows, cols], hss.at[n, stage], hrs.at[n, stage], pdev)

    g_forward(0)
    for c in local[3:5]:
        c.wait()
    core_send(0)
    for rz in (1, 3):
        z_landed(rz)
        x_near(rz)
    g_forward(1)
    g_send(0, 3)
    g_send(1, 3)
    core_wait(0)
    pre_forward(0)
    x_pass(1)
    x_pass(3)
    g_forward(2)
    w_core(0)
    core_send(1)
    core_send(3)
    g_last(0)
    for c in local[5:]:
        c.wait()
    w_wait(0)
    partner(0, 0)
    g_forward(3)
    z_landed(2)
    x_near(2)
    core_wait(1)
    pre_forward(1)
    w_core(1)
    own(0)
    x_pass(2)
    g_last(1)
    partner(1, 0)
    w_wait(1)
    partner(0, 1)
    partner(1, 1)
    core_send(2)
    core_wait(3)
    pre_forward(3)
    own(1)
    core_wait(2)
    pre_forward(2)
    for hk in range(2):
        lanes = slice(hk * HD, (hk + 1) * HD)
        vv = vbuf[:, :, :, :, lanes].reshape(PRE, HD)
        ot[hk] = dot(vv, ebuf[hk].reshape(PRE, QW), ((0,), (0,))) + dot(vd[:, lanes], edoc[hk], ((0,), (0,)))
    for n in range(2):
        cols = pl.ds(n * 256, 256)
        for stage in range(2):
            rows = pl.ds(stage * 256, 256)
            landed(hr.at[rows, cols], hss.at[n, stage], hrs.at[n, stage])
        hgt[:, cols] += hr[:, cols].astype(F32)

    for hd in range(4):
        hk, cols = hd // 2, slice((hd % 2) * TOK, (hd % 2 + 1) * TOK)
        g = hgt[hd * HD : (hd + 1) * HD, :].astype(BF16).astype(F32)
        inv = 1.0 / jnp.sum(lsum[hk, :, cols], axis=0, keepdims=True)
        scaled = (g * inv).astype(BF16)
        drow[hk, :, cols] = jnp.sum(g * ot[hk, :, cols], axis=0, keepdims=True) * (inv * inv)
        dot_t[hk, :, cols] = scaled
        dos[hk, cols, :] = scaled.T

    def put_terms(a, hk, rz, t):
        t = t.astype(BF16).reshape(4, 2, 64, HD)
        for rc in range(2):
            pb[rz, a, rc, :, :, hk * HD : (hk + 1) * HD] = t[:, rc]

    def dv_block(rz):
        for hk in range(2):
            put_terms(0, hk, rz, dot(ebuf[hk, :, :, rz].reshape(QR, QW), dos[hk]))
        pair_send(rz, 0)

    def logit_grads(vv, hk, s, cols):
        dp = dot(vv, dot_t[hk, :, cols]) - drow[hk, :, cols]
        return (s.astype(F32) * dp).astype(BF16)

    def dk_block(rz):
        for hk in range(2):
            vv = vbuf[:, :, rz, :, hk * HD : (hk + 1) * HD].reshape(QR, HD)
            for n in range(2):
                cols = slice(n * TOK, (n + 1) * TOK)
                ds = logit_grads(vv, hk, sbuf[hk, :, :, rz, :, cols].reshape(QR, TOK), cols)
                sbuf[hk, :, :, rz, :, cols] = ds.reshape(4, 2, 64, TOK)
            put_terms(1, hk, rz, dot(sbuf[hk, :, :, rz].reshape(QR, QW), qs[hk]) * SCALE)
        pair_send(rz, 1)

    def pair_send(rz, a):
        send(pb.at[rz, a, 1], pr.at[rz, a], ps.at[rz, a], prs.at[rz, a], other)

    def pair_sum(rz, a, rx):
        return pb[rz, a, 0, rx].astype(F32) + pr[rz, a, rx].astype(F32)

    def pair_wait(rz, a):
        landed(pr.at[rz, a], ps.at[rz, a], prs.at[rz, a])

    def z_first(rz):
        n = rz // 2
        pair_wait(rz, 0)
        for rx in range(4):
            vs[n, rx] = pair_sum(rz, 0, rx).astype(BF16)
        send(vs.at[n], vr.at[n], vss.at[n], vrs.at[n], zdev[rz])

    def stay(a, rx):
        t = pair_sum(0, a, rx)
        return t if a else t + vr[0, rx].astype(F32) + vr[1, rx].astype(F32)

    def x_send(rz, a):
        pair_wait(rz, a)
        if rz == 0 and a == 0:
            for n in range(2):
                landed(vr.at[n], vss.at[n], vrs.at[n])
        for rx in (2, 1, 3):
            n = rx - 1
            t = pair_sum(rz, a, rx) if rz else stay(a, rx)
            xs[rz, a, n] = t.astype(BF16)
            send(xs.at[rz, a, n], xr.at[rz, a, n], xss.at[rz, a, n], xrs.at[rz, a, n], xdev[rx - 4])

    def x_total(rz, a):
        t = pair_sum(rz, a, 0) if rz else stay(a, 0)
        for n in range(3):
            landed(xr.at[rz, a, n], xss.at[rz, a, n], xrs.at[rz, a, n])
            t = t + xr[rz, a, n].astype(F32)
        if rz:
            zs[rz - 1, a] = t.astype(BF16)
            send(zs.at[rz - 1, a], zr.at[rz - 1, a], zss.at[rz - 1, a], zrs.at[rz - 1, a], zdev[rz])
        else:
            tacc[a] = t

    outs = []

    def put(src, dst, n):
        c = pltpu.make_async_copy(src, dst, osem.at[n])
        c.start()
        outs.append(c)

    def z_total(a, out, dst):
        t = tacc[a]
        for n in (1, 0, 2) if a else (1,):
            landed(zr.at[n, a], zss.at[n, a], zrs.at[n, a])
            t = t + zr[n, a].astype(F32)
        out[...] = t.astype(BF16)
        put(out, dst, a)

    dv_block(1)
    dv_block(3)
    dv_block(2)
    z_first(1)
    dk_block(2)
    z_first(3)
    x_send(2, 0)
    dk_block(1)
    x_send(2, 1)
    dk_block(3)
    x_send(1, 1)
    dv_block(0)
    x_send(3, 1)
    dk_block(0)
    x_total(2, 0)
    x_total(2, 1)

    def doc_backward(hk):
        lanes = slice(hk * HD, (hk + 1) * HD)
        for n in range(2):
            cols = slice(n * TOK, (n + 1) * TOK)
            sdoc[hk, :, cols] = logit_grads(vd[:, lanes], hk, sdoc[hk, :, cols], cols)
        odk[:, lanes] = (dot(sdoc[hk], qs[hk]) * SCALE).astype(BF16)
        odv[:, lanes] = dot(edoc[hk], dos[hk]).astype(BF16)

    doc_backward(0)
    x_send(0, 1)
    x_total(1, 1)
    x_total(3, 1)
    doc_backward(1)
    x_send(0, 0)
    put(odk, dk_hbm, 2)
    put(odv, dv_hbm, 3)

    for hk in range(2):
        lanes = slice(hk * HD, (hk + 1) * HD)
        kk = kbuf[:, :, :, :, lanes].reshape(PRE, HD)
        t = dot(kk, sbuf[hk].reshape(PRE, QW), ((0,), (0,))) + dot(kd[:, lanes], sdoc[hk], ((0,), (0,)))
        for g in range(2):
            hd = hk * 2 + g
            odq[:, hd * HD : (hd + 1) * HD] = (t[:, g * TOK : (g + 1) * TOK] * SCALE).astype(BF16).T
    put(odq, dq_hbm, 4)
    x_total(0, 1)
    z_total(1, opk, pdk_hbm)
    x_total(0, 0)
    z_total(0, opv, pdv_hbm)
    for c in started:
        c.wait_send()
    for c in outs:
        c.wait()


def finish(*refs):
    ins, outs, held, sem = refs[:5], refs[5:10], refs[10:15], refs[15]
    into = [pltpu.make_async_copy(a, b, sem.at[0, i]) for i, (a, b) in enumerate(zip(ins, held))]
    back = [pltpu.make_async_copy(a, b, sem.at[1, i]) for i, (a, b) in enumerate(zip(held, outs))]
    for c in into:
        c.start()
    for a, b in zip(into, back):
        a.wait()
        b.start()
    for c in back:
        c.wait()


def on_device(queries, keys, values, prefix_keys, prefix_values, out_grad, out_weight, doc_lengths):
    sd = jax.ShapeDtypeStruct
    hbm = pl.BlockSpec(memory_space=pl.ANY)
    vm = pltpu.VMEM
    dma = pltpu.SemaphoreType.DMA
    shapes = (
        sd((TOK, 512), BF16),
        sd((TOK, 256), BF16),
        sd((TOK, 256), BF16),
        sd((64, 256), BF16),
        sd((64, 256), BF16),
    )
    grads = pl.pallas_call(
        kernel,
        out_shape=shapes,
        in_specs=[pl.BlockSpec(memory_space=pltpu.SMEM)] + [hbm] * 7,
        out_specs=(hbm,) * 5,
        scratch_shapes=[
            vm((TOK, 512), BF16),
            vm((TOK, 256), BF16),
            vm((TOK, 256), BF16),
            vm((LAY, TOK), BF16),
            vm((512, LAY), BF16),
            vm((512, LAY), BF16),
            vm((512, TOK), BF16),
            vm((512, TOK), BF16),
            vm((4, 2, 4, 64, 256), BF16),
            vm((4, 2, 4, 64, 256), BF16),
            vm((2, 4, 2, 4, 64, QW), BF16),
            vm((2, 4, 2, 4, 64, QW), BF16),
            vm((2, TOK, QW), BF16),
            vm((2, TOK, QW), BF16),
            vm((2, HD, QW), BF16),
            vm((2, QW, HD), BF16),
            vm((2, HD, QW), BF16),
            vm((2, QW, HD), BF16),
            vm((2, HD, QW), F32),
            vm((2, 8, QW), F32),
            vm((2, 1, QW), F32),
            vm((512, TOK), F32),
            vm((4, 2, 2, 4, 64, 256), BF16),
            vm((4, 2, 4, 64, 256), BF16),
            vm((2, 4, 64, 256), BF16),
            vm((2, 4, 64, 256), BF16),
            vm((4, 2, 3, 64, 256), BF16),
            vm((4, 2, 3, 64, 256), BF16),
            vm((2, 64, 256), F32),
            vm((3, 2, 64, 256), BF16),
            vm((3, 2, 64, 256), BF16),
            vm((TOK, 512), BF16),
            vm((TOK, 256), BF16),
            vm((TOK, 256), BF16),
            vm((64, 256), BF16),
            vm((64, 256), BF16),
            dma((7,)),
            dma((3, NC)),
            dma((3, NC)),
            dma((2, 2)),
            dma((2, 2)),
            dma((2, 2)),
            dma((2, 2)),
            dma((2,)),
            dma((2,)),
            dma((2, 3)),
            dma((2, 3)),
            dma((2, 4, 3)),
            dma((2, 4, 3)),
            dma((2, 4)),
            dma((2, 4)),
            dma((4, 2)),
            dma((4, 2)),
            dma((2,)),
            dma((2,)),
            dma((4, 2, 3)),
            dma((4, 2, 3)),
            dma((3, 2)),
            dma((3, 2)),
            dma((5,)),
        ],
        compiler_params=pltpu.CompilerParams(
            collective_id=0, has_side_effects=True, vmem_limit_bytes=60 * 1024 * 1024
        ),
    )(doc_lengths, queries, keys, values, prefix_keys, prefix_values, out_grad.T, out_weight)
    return pl.pallas_call(
        finish,
        out_shape=shapes,
        in_specs=[hbm] * 5,
        out_specs=(hbm,) * 5,
        scratch_shapes=[vm(s.shape, s.dtype) for s in shapes] + [dma((2, 5))],
    )(*grads)


def solution(mesh):
    return jax.shard_map(
        on_device,
        mesh=mesh,
        in_specs=(P("docs", "heads"),) * 6 + (P("heads", None), P("docs", None)),
        out_specs=(P("docs", "heads"),) * 5,
        check_vma=False,
    )
```

```python
import jax
import jax.numpy as jnp
from jax import lax
from jax.experimental import pallas as pl
from jax.experimental.pallas import tpu as pltpu
from jax.sharding import PartitionSpec as P

HD = 128
SOFTCAP = 50.0
SCALE = 1.0 / 12.0
LOG2E = 1.4426950408889634
F32 = jnp.float32
BF16 = jnp.bfloat16
MESH = pl.DeviceIdType.MESH

TOK = 512
FEAT = 576
LAY = 4 * FEAT
NC = 4
CH = TOK // NC
QW = 1024
PRE = 2048
QR = 512


def dot(a, b, dims=((1,), (0,))):
    return lax.dot_general(a, b, (dims, ((), ())), preferred_element_type=F32)


def kernel(
    len_ref, q_hbm, k_hbm, v_hbm, pk_hbm, pv_hbm, og_hbm, w_hbm,
    dq_hbm, dk_hbm, dv_hbm, pdk_hbm, pdv_hbm,
    qb, kd, vd, gl, wl, wp, hs, hr, kbuf, vbuf, ebuf, sbuf, edoc, sdoc, qt, qs, dot_t, dos, ot, lsum, drow, hgt,
    pb, pr, vs, vr, xs, xr, tacc, zs, zr, odq, odk, odv, opk, opv,
    ls, gs, gr, hss, hrs, wzs, wzr, wcs, wcr, kzs, kzr, kxs, kxr, kcs, kcr, ps, prs, vss, vrs, xss, xrs, zss, zrs, osem,
):
    d = lax.axis_index("docs")
    h = lax.axis_index("heads")
    core = lax.rem(d, 2)
    x = lax.rem(d // 2, 4)
    zh = d // 8
    zl = h // 4
    y = lax.rem(h, 4)

    def doc_id(zz, xx, cc):
        return {"docs": (lax.rem(zz + 4, 4) * 4 + lax.rem(xx + 4, 4)) * 2 + cc}

    def head_id(zz, yy):
        return {"heads": zz * 4 + lax.rem(yy + 4, 4)}

    other = doc_id(zh, x, 1 - core)
    xdev = {1: doc_id(zh, x + 1, core), -1: doc_id(zh, x - 1, core), -2: doc_id(zh, x - 2, core)}
    xdev[-3] = xdev[1]
    zdev = {1: doc_id(zh + 1, x, core), 2: doc_id(zh + 2, x, core), 3: doc_id(zh + 3, x, core)}
    ydev = {1: head_id(zl, y + 1), -1: head_id(zl, y - 1)}
    pdev = head_id(1 - zl, y)
    zz = lax.rem(zh + 2 * zl + 3, 4)
    wdev = {"docs": (zz * 4 + x) * 2 + core, "heads": (1 - zl) * 4 + y}

    barrier = pltpu.get_barrier_semaphore()
    peers = (other, xdev[1], xdev[-1], xdev[-2], zdev[1], zdev[2], zdev[3], ydev[1], ydev[-1], pdev, wdev)
    for p in peers:
        pl.semaphore_signal(barrier, inc=1, device_id=p, device_id_type=MESH)

    def g_rows(ry):
        return pl.ds(pl.multiple_of(lax.rem(y + ry + 4, 4) * FEAT, FEAT), FEAT)

    def layer(zz):
        return pl.ds(pl.multiple_of(zz * LAY, LAY), LAY)

    local = [
        pltpu.make_async_copy(q_hbm, qb, ls.at[0]),
        pltpu.make_async_copy(k_hbm, kd, ls.at[1]),
        pltpu.make_async_copy(v_hbm, vd, ls.at[2]),
        pltpu.make_async_copy(pk_hbm, kbuf.at[0, 0, 0], ls.at[3]),
        pltpu.make_async_copy(pv_hbm, vbuf.at[0, 0, 0], ls.at[4]),
        pltpu.make_async_copy(og_hbm, gl.at[g_rows(0)], ls.at[5]),
        pltpu.make_async_copy(w_hbm.at[:, layer(zl)], wl, ls.at[6]),
    ]
    for c in local:
        c.start()
    pl.semaphore_wait(barrier, len(peers))

    started = []

    def remote(src, dst, ssem, rsem, device):
        return pltpu.make_async_remote_copy(
            src_ref=src, dst_ref=dst, send_sem=ssem, recv_sem=rsem, device_id=device, device_id_type=MESH
        )

    def send(*args):
        c = remote(*args)
        c.start()
        started.append(c)

    def landed(dst, ssem, rsem):
        remote(dst, dst, ssem, rsem, other).wait_recv()

    def g_route(kind, c):
        s = 1 if c % 2 == 0 else -1
        return ((0, ydev[s], -s), (0, ydev[-s], s), (s, ydev[-s], 2))[kind]

    def g_send(kind, c):
        ry, to, _ = g_route(kind, c)
        cols = pl.ds(c * CH, CH)
        at = gl.at[g_rows(ry), cols]
        send(og_hbm.at[:, cols] if kind < 2 else at, at, gs.at[kind, c], gr.at[kind, c], to)

    def g_wait(kind, c):
        landed(gl.at[g_rows(g_route(kind, c)[2]), pl.ds(c * CH, CH)], gs.at[kind, c], gr.at[kind, c])

    def g_forward(c):
        g_wait(1, c)
        g_send(2, c)

    def w_rows(stage, rc, part):
        first = stage * 256 + (core if rc == 0 else 1 - core) * 128
        if part is None:
            return pl.ds(pl.multiple_of(first, 128), 128)
        return pl.ds(pl.multiple_of(first + part * 64, 64), 64)

    def w_send(stage):
        for part, to in ((0, pdev), (1, wdev)):
            rows = w_rows(stage, 0, part)
            send(w_hbm.at[rows, layer(1 - zl)], wp.at[rows], wzs.at[stage, part], wzr.at[stage, part], to)

    def w_core(stage):
        for part in range(2):
            landed(wp.at[w_rows(stage, 0, part)], wzs.at[stage, part], wzr.at[stage, part])
        rows = w_rows(stage, 0, None)
        send(wp.at[rows], wp.at[rows], wcs.at[stage], wcr.at[stage], other)

    def w_wait(stage):
        landed(wp.at[w_rows(stage, 1, None)], wcs.at[stage], wcr.at[stage])

    pre = ((0, kbuf, pk_hbm), (1, vbuf, pv_hbm))
    for i, buf, src in pre:
        send(src, buf.at[0, 0, 3], kzs.at[i, 2], kzr.at[i, 2], zdev[1])
        send(src, buf.at[0, 0, 1], kzs.at[i, 0], kzr.at[i, 0], zdev[3])
    w_send(0)
    for i, buf, src in pre:
        for rx in (1, 3, 2):
            send(src, buf.at[rx, 0, 0], kxs.at[i, 0, rx - 1], kxr.at[i, 0, rx - 1], xdev[-rx])
    for c in range(3):
        g_send(0, c)
        g_send(1, c)
    for c in local[:3]:
        c.wait()
    for hd in range(4):
        blk = qb[:, hd * HD : (hd + 1) * HD]
        qs[hd // 2, (hd % 2) * TOK : (hd % 2 + 1) * TOK, :] = blk
        qt[hd // 2, :, (hd % 2) * TOK : (hd % 2 + 1) * TOK] = blk.T

    b0 = len_ref[0, 0]
    b1 = b0 + len_ref[0, 1]
    b2 = b1 + len_ref[0, 2]

    def segment(p):
        return (p >= b0).astype(jnp.int32) + (p >= b1).astype(jnp.int32) + (p >= b2).astype(jnp.int32)

    def weights(kk, hk, cols, mask):
        t = jnp.tanh(dot(kk, qt[hk, :, cols]) * (SCALE / SOFTCAP))
        e = jnp.exp2(t * (SOFTCAP * LOG2E))
        if mask is not None:
            e = jnp.where(mask, e, 0.0)
        return e, e * (1.0 - t * t)

    def partial_sums(e):
        return jnp.sum(e.reshape(e.shape[0] // 8, 8, e.shape[1]), axis=0)

    def doc_forward(hk):
        lsum[hk] = jnp.zeros((8, QW), F32)
        for j in range(4):
            rows = slice(j * HD, (j + 1) * HD)
            lo, hi = j * HD, min(TOK, (j + 3) * HD)
            key = lo + lax.broadcasted_iota(jnp.int32, (HD, hi - lo), 0)
            row = lo + lax.broadcasted_iota(jnp.int32, (HD, hi - lo), 1)
            mask = (key <= row) & (segment(key) == segment(row))
            for g in range(2):
                cols = slice(g * TOK + lo, g * TOK + hi)
                e, s = weights(kd[rows, hk * HD : (hk + 1) * HD], hk, cols, mask)
                lsum[hk, :, cols] += partial_sums(e)
                edoc[hk, rows, cols] = e.astype(BF16)
                sdoc[hk, rows, cols] = s.astype(BF16)
                for a, b in ((0, lo), (hi, TOK)):
                    if a < b:
                        edoc[hk, rows, g * TOK + a : g * TOK + b] = jnp.zeros((HD, b - a), BF16)
                        sdoc[hk, rows, g * TOK + a : g * TOK + b] = jnp.zeros((HD, b - a), BF16)

    def pre_forward(rz):
        def one(hk, carry):
            lanes = pl.ds(pl.multiple_of(hk * HD, HD), HD)
            e, s = weights(kbuf[:, :, rz, :, lanes].reshape(QR, HD), hk, slice(None), None)
            lsum[hk] += partial_sums(e)
            ebuf[hk, :, :, rz] = e.astype(BF16).reshape(4, 2, 64, QW)
            sbuf[hk, :, :, rz] = s.astype(BF16).reshape(4, 2, 64, QW)
            return carry

        lax.fori_loop(0, 2, one, 0)

    def z_landed(rz):
        for i, buf, _ in pre:
            landed(buf.at[0, 0, rz], kzs.at[i, rz - 1], kzr.at[i, rz - 1])

    def x_near(rz):
        for i, buf, _ in pre:
            for rx in (1, 3, 2) if rz == 2 else (1, 3):
                send(buf.at[0, 0, rz], buf.at[rx, 0, rz], kxs.at[i, rz, rx - 1], kxr.at[i, rz, rx - 1], xdev[-rx])

    def x_landed(i, rx, rz):
        landed(pre[i][1].at[rx, 0, rz], kxs.at[i, rz, rx - 1], kxr.at[i, rz, rx - 1])

    def x_pass(rz):
        for i, got, to in ((0, 3, 1), (1, 1, -1)):
            x_landed(i, got, rz)
            buf = pre[i][1]
            send(buf.at[got, 0, rz], buf.at[2, 0, rz], kxs.at[i, rz, 1], kxr.at[i, rz, 1], xdev[to])

    def core_send(rz):
        for i, buf, _ in pre:
            for rx in (1, 3, 2):
                if rz in (0, 2) or rx == 2 or rx == (1, 3)[i]:
                    x_landed(i, rx, rz)
            send(buf.at[:, 0, rz], buf.at[:, 1, rz], kcs.at[i, rz], kcr.at[i, rz], other)

    def core_wait(rz):
        for i, buf, _ in pre:
            landed(buf.at[:, 1, rz], kcs.at[i, rz], kcr.at[i, rz])

    doc_forward(0)
    doc_forward(1)

    def project(w, n):
        return dot(w, gl[:, n * 256 : (n + 1) * 256])

    def g_last(n):
        for c in (2 * n, 2 * n + 1):
            g_wait(0, c)
            g_wait(2, c)

    def own(n):
        hgt[:, n * 256 : (n + 1) * 256] = project(wl[...], n)

    def partner(n, stage):
        rows = pl.ds(stage * 256, 256)
        cols = pl.ds(n * 256, 256)
        hs[rows, cols] = project(wp[rows, :], n).astype(BF16)
        send(hs.at[rows, cols], hr.at[rows, cols], hss.at[n, stage], hrs.at[n, stage], pdev)

    g_forward(0)
    for c in local[3:5]:
        c.wait()
    core_send(0)
    for rz in (1, 3):
        z_landed(rz)
    for i, buf, _ in pre:
        send(buf.at[0, 0, 3 - 2 * i], buf.at[0, 0, 2], kzs.at[i, 1], kzr.at[i, 1], zdev[1 + 2 * i])
    w_send(1)
    for rz in (1, 3):
        x_near(rz)
    g_forward(1)
    g_send(0, 3)
    g_send(1, 3)
    core_wait(0)
    pre_forward(0)
    x_pass(1)
    x_pass(3)
    g_forward(2)
    w_core(0)
    core_send(1)
    core_send(3)
    g_last(0)
    for c in local[5:]:
        c.wait()
    w_wait(0)
    partner(0, 0)
    g_forward(3)
    z_landed(2)
    x_near(2)
    core_wait(1)
    pre_forward(1)
    w_core(1)
    own(0)
    w_wait(1)
    partner(0, 1)
    g_last(1)
    partner(1, 0)
    partner(1, 1)
    core_wait(3)
    pre_forward(3)
    own(1)
    core_send(2)
    core_wait(2)
    pre_forward(2)
    for hk in range(2):
        lanes = slice(hk * HD, (hk + 1) * HD)
        vv = vbuf[:, :, :, :, lanes].reshape(PRE, HD)
        ot[hk] = dot(vv, ebuf[hk].reshape(PRE, QW), ((0,), (0,))) + dot(vd[:, lanes], edoc[hk], ((0,), (0,)))
    for n in range(2):
        cols = pl.ds(n * 256, 256)
        for stage in range(2):
            rows = pl.ds(stage * 256, 256)
            landed(hr.at[rows, cols], hss.at[n, stage], hrs.at[n, stage])
        hgt[:, cols] += hr[:, cols].astype(F32)

    for hd in range(4):
        hk, cols = hd // 2, slice((hd % 2) * TOK, (hd % 2 + 1) * TOK)
        g = hgt[hd * HD : (hd + 1) * HD, :].astype(BF16).astype(F32)
        inv = 1.0 / jnp.sum(lsum[hk, :, cols], axis=0, keepdims=True)
        scaled = (g * inv).astype(BF16)
        drow[hk, :, cols] = jnp.sum(g * ot[hk, :, cols], axis=0, keepdims=True) * (inv * inv)
        dot_t[hk, :, cols] = scaled
        dos[hk, cols, :] = scaled.T

    def put_terms(a, hk, rz, t):
        t = t.astype(BF16).reshape(4, 2, 64, HD)
        for rc in range(2):
            pb[rz, a, rc, :, :, hk * HD : (hk + 1) * HD] = t[:, rc]

    def dv_block(rz):
        for hk in range(2):
            put_terms(0, hk, rz, dot(ebuf[hk, :, :, rz].reshape(QR, QW), dos[hk]))
        pair_send(rz, 0)

    def logit_grads(vv, hk, s, cols):
        dp = dot(vv, dot_t[hk, :, cols]) - drow[hk, :, cols]
        return (s.astype(F32) * dp).astype(BF16)

    def dk_block(rz):
        for hk in range(2):
            vv = vbuf[:, :, rz, :, hk * HD : (hk + 1) * HD].reshape(QR, HD)
            for n in range(2):
                cols = slice(n * TOK, (n + 1) * TOK)
                ds = logit_grads(vv, hk, sbuf[hk, :, :, rz, :, cols].reshape(QR, TOK), cols)
                sbuf[hk, :, :, rz, :, cols] = ds.reshape(4, 2, 64, TOK)
            put_terms(1, hk, rz, dot(sbuf[hk, :, :, rz].reshape(QR, QW), qs[hk]) * SCALE)
        pair_send(rz, 1)

    def pair_send(rz, a):
        send(pb.at[rz, a, 1], pr.at[rz, a], ps.at[rz, a], prs.at[rz, a], other)

    def pair_sum(rz, a, rx):
        return pb[rz, a, 0, rx].astype(F32) + pr[rz, a, rx].astype(F32)

    def pair_wait(rz, a):
        landed(pr.at[rz, a], ps.at[rz, a], prs.at[rz, a])

    def z_first(rz):
        n = rz // 2
        pair_wait(rz, 0)
        for rx in range(4):
            vs[n, rx] = pair_sum(rz, 0, rx).astype(BF16)
        send(vs.at[n], vr.at[n], vss.at[n], vrs.at[n], zdev[rz])

    def stay(a, rx):
        t = pair_sum(0, a, rx)
        return t if a else t + vr[0, rx].astype(F32) + vr[1, rx].astype(F32)

    def x_send(rz, a):
        pair_wait(rz, a)
        if rz == 0 and a == 0:
            for n in range(2):
                landed(vr.at[n], vss.at[n], vrs.at[n])
        for rx in (2, 1, 3):
            n = rx - 1
            t = pair_sum(rz, a, rx) if rz else stay(a, rx)
            xs[rz, a, n] = t.astype(BF16)
            send(xs.at[rz, a, n], xr.at[rz, a, n], xss.at[rz, a, n], xrs.at[rz, a, n], xdev[rx - 4])

    def x_total(rz, a):
        t = pair_sum(rz, a, 0) if rz else stay(a, 0)
        for n in range(3):
            landed(xr.at[rz, a, n], xss.at[rz, a, n], xrs.at[rz, a, n])
            t = t + xr[rz, a, n].astype(F32)
        if rz:
            zs[rz - 1, a] = t.astype(BF16)
            send(zs.at[rz - 1, a], zr.at[rz - 1, a], zss.at[rz - 1, a], zrs.at[rz - 1, a], zdev[rz])
        else:
            tacc[a] = t

    outs = []

    def put(src, dst, n):
        c = pltpu.make_async_copy(src, dst, osem.at[n])
        c.start()
        outs.append(c)

    def z_total(a, out, dst):
        t = tacc[a]
        for n in (1, 0, 2) if a else (1,):
            landed(zr.at[n, a], zss.at[n, a], zrs.at[n, a])
            t = t + zr[n, a].astype(F32)
        out[...] = t.astype(BF16)
        put(out, dst, a)

    dv_block(1)
    dv_block(3)
    dv_block(2)
    z_first(1)
    dk_block(2)
    z_first(3)
    x_send(2, 0)
    dk_block(1)
    x_send(2, 1)
    dk_block(3)
    x_send(1, 1)
    dv_block(0)
    x_send(3, 1)
    dk_block(0)
    x_total(2, 0)
    x_total(2, 1)

    def doc_backward(hk):
        lanes = slice(hk * HD, (hk + 1) * HD)
        for n in range(2):
            cols = slice(n * TOK, (n + 1) * TOK)
            sdoc[hk, :, cols] = logit_grads(vd[:, lanes], hk, sdoc[hk, :, cols], cols)
        odk[:, lanes] = (dot(sdoc[hk], qs[hk]) * SCALE).astype(BF16)
        odv[:, lanes] = dot(edoc[hk], dos[hk]).astype(BF16)

    doc_backward(0)
    x_send(0, 1)
    x_total(1, 1)
    x_total(3, 1)
    x_send(0, 0)
    doc_backward(1)
    put(odk, dk_hbm, 2)
    put(odv, dv_hbm, 3)

    for hk in range(2):
        lanes = slice(hk * HD, (hk + 1) * HD)
        kk = kbuf[:, :, :, :, lanes].reshape(PRE, HD)
        t = dot(kk, sbuf[hk].reshape(PRE, QW), ((0,), (0,))) + dot(kd[:, lanes], sdoc[hk], ((0,), (0,)))
        for g in range(2):
            hd = hk * 2 + g
            odq[:, hd * HD : (hd + 1) * HD] = (t[:, g * TOK : (g + 1) * TOK] * SCALE).astype(BF16).T
    put(odq, dq_hbm, 4)
    x_total(0, 1)
    z_total(1, opk, pdk_hbm)
    x_total(0, 0)
    z_total(0, opv, pdv_hbm)
    for c in started:
        c.wait_send()
    for c in outs:
        c.wait()


def finish(*refs):
    ins, outs, held, sem = refs[:5], refs[5:10], refs[10:15], refs[15]
    into = [pltpu.make_async_copy(a, b, sem.at[0, i]) for i, (a, b) in enumerate(zip(ins, held))]
    back = [pltpu.make_async_copy(a, b, sem.at[1, i]) for i, (a, b) in enumerate(zip(held, outs))]
    for c in into:
        c.start()
    for a, b in zip(into, back):
        a.wait()
        b.start()
    for c in back:
        c.wait()


def on_device(queries, keys, values, prefix_keys, prefix_values, out_grad, out_weight, doc_lengths):
    sd = jax.ShapeDtypeStruct
    hbm = pl.BlockSpec(memory_space=pl.ANY)
    vm = pltpu.VMEM
    dma = pltpu.SemaphoreType.DMA
    shapes = (
        sd((TOK, 512), BF16),
        sd((TOK, 256), BF16),
        sd((TOK, 256), BF16),
        sd((64, 256), BF16),
        sd((64, 256), BF16),
    )
    grads = pl.pallas_call(
        kernel,
        out_shape=shapes,
        in_specs=[pl.BlockSpec(memory_space=pltpu.SMEM)] + [hbm] * 7,
        out_specs=(hbm,) * 5,
        scratch_shapes=[
            vm((TOK, 512), BF16),
            vm((TOK, 256), BF16),
            vm((TOK, 256), BF16),
            vm((LAY, TOK), BF16),
            vm((512, LAY), BF16),
            vm((512, LAY), BF16),
            vm((512, TOK), BF16),
            vm((512, TOK), BF16),
            vm((4, 2, 4, 64, 256), BF16),
            vm((4, 2, 4, 64, 256), BF16),
            vm((2, 4, 2, 4, 64, QW), BF16),
            vm((2, 4, 2, 4, 64, QW), BF16),
            vm((2, TOK, QW), BF16),
            vm((2, TOK, QW), BF16),
            vm((2, HD, QW), BF16),
            vm((2, QW, HD), BF16),
            vm((2, HD, QW), BF16),
            vm((2, QW, HD), BF16),
            vm((2, HD, QW), F32),
            vm((2, 8, QW), F32),
            vm((2, 1, QW), F32),
            vm((512, TOK), F32),
            vm((4, 2, 2, 4, 64, 256), BF16),
            vm((4, 2, 4, 64, 256), BF16),
            vm((2, 4, 64, 256), BF16),
            vm((2, 4, 64, 256), BF16),
            vm((4, 2, 3, 64, 256), BF16),
            vm((4, 2, 3, 64, 256), BF16),
            vm((2, 64, 256), F32),
            vm((3, 2, 64, 256), BF16),
            vm((3, 2, 64, 256), BF16),
            vm((TOK, 512), BF16),
            vm((TOK, 256), BF16),
            vm((TOK, 256), BF16),
            vm((64, 256), BF16),
            vm((64, 256), BF16),
            dma((7,)),
            dma((3, NC)),
            dma((3, NC)),
            dma((2, 2)),
            dma((2, 2)),
            dma((2, 2)),
            dma((2, 2)),
            dma((2,)),
            dma((2,)),
            dma((2, 3)),
            dma((2, 3)),
            dma((2, 4, 3)),
            dma((2, 4, 3)),
            dma((2, 4)),
            dma((2, 4)),
            dma((4, 2)),
            dma((4, 2)),
            dma((2,)),
            dma((2,)),
            dma((4, 2, 3)),
            dma((4, 2, 3)),
            dma((3, 2)),
            dma((3, 2)),
            dma((5,)),
        ],
        compiler_params=pltpu.CompilerParams(
            collective_id=0, has_side_effects=True, vmem_limit_bytes=60 * 1024 * 1024
        ),
    )(doc_lengths, queries, keys, values, prefix_keys, prefix_values, out_grad.T, out_weight)
    return pl.pallas_call(
        finish,
        out_shape=shapes,
        in_specs=[hbm] * 5,
        out_specs=(hbm,) * 5,
        scratch_shapes=[vm(s.shape, s.dtype) for s in shapes] + [dma((2, 5))],
    )(*grads)


def solution(mesh):
    return jax.shard_map(
        on_device,
        mesh=mesh,
        in_specs=(P("docs", "heads"),) * 6 + (P("heads", None), P("docs", None)),
        out_specs=(P("docs", "heads"),) * 5,
        check_vma=False,
    )
```

```python
import jax
import jax.numpy as jnp
from jax import lax
from jax.experimental import pallas as pl
from jax.experimental.pallas import tpu as pltpu
from jax.sharding import PartitionSpec as P

HD = 128
SOFTCAP = 50.0
SCALE = 1.0 / 12.0
LOG2E = 1.4426950408889634
F32 = jnp.float32
BF16 = jnp.bfloat16
MESH = pl.DeviceIdType.MESH

TOK = 512
FEAT = 576
LAY = 4 * FEAT
NC = 4
CH = TOK // NC
QW = 1024
PRE = 2048
QR = 512


def dot(a, b, dims=((1,), (0,))):
    return lax.dot_general(a, b, (dims, ((), ())), preferred_element_type=F32)


def kernel(
    len_ref, q_hbm, k_hbm, v_hbm, pk_hbm, pv_hbm, og_hbm, w_hbm,
    dq_hbm, dk_hbm, dv_hbm, pdk_hbm, pdv_hbm,
    qb, kd, vd, gl, wl, wp, hs, hr, kbuf, vbuf, ebuf, sbuf, edoc, sdoc, qt, qs, dot_t, dos, ot, lsum, drow, hgt,
    pb, pr, vs, vr, xs, xr, tacc, zs, zr, odq, odk, odv, opk, opv,
    ls, gs, gr, hss, hrs, wzs, wzr, wcs, wcr, kzs, kzr, kxs, kxr, kcs, kcr, ps, prs, vss, vrs, xss, xrs, zss, zrs, osem,
):
    d = lax.axis_index("docs")
    h = lax.axis_index("heads")
    core = lax.rem(d, 2)
    x = lax.rem(d // 2, 4)
    zh = d // 8
    zl = h // 4
    y = lax.rem(h, 4)

    def doc_id(zz, xx, cc):
        return {"docs": (lax.rem(zz + 4, 4) * 4 + lax.rem(xx + 4, 4)) * 2 + cc}

    def head_id(zz, yy):
        return {"heads": zz * 4 + lax.rem(yy + 4, 4)}

    other = doc_id(zh, x, 1 - core)
    xdev = {1: doc_id(zh, x + 1, core), -1: doc_id(zh, x - 1, core), -2: doc_id(zh, x - 2, core)}
    xdev[-3] = xdev[1]
    zdev = {1: doc_id(zh + 1, x, core), 2: doc_id(zh + 2, x, core), 3: doc_id(zh + 3, x, core)}
    ydev = {1: head_id(zl, y + 1), -1: head_id(zl, y - 1)}
    pdev = head_id(1 - zl, y)
    zz = lax.rem(zh + 2 * zl + 3, 4)
    wdev = {"docs": (zz * 4 + x) * 2 + core, "heads": (1 - zl) * 4 + y}

    barrier = pltpu.get_barrier_semaphore()
    peers = (other, xdev[1], xdev[-1], xdev[-2], zdev[1], zdev[2], zdev[3], ydev[1], ydev[-1], pdev, wdev)
    for p in peers:
        pl.semaphore_signal(barrier, inc=1, device_id=p, device_id_type=MESH)

    def g_rows(ry):
        return pl.ds(pl.multiple_of(lax.rem(y + ry + 4, 4) * FEAT, FEAT), FEAT)

    def layer(zz):
        return pl.ds(pl.multiple_of(zz * LAY, LAY), LAY)

    local = [
        pltpu.make_async_copy(q_hbm, qb, ls.at[0]),
        pltpu.make_async_copy(k_hbm, kd, ls.at[1]),
        pltpu.make_async_copy(v_hbm, vd, ls.at[2]),
        pltpu.make_async_copy(pk_hbm, kbuf.at[0, 0, 0], ls.at[3]),
        pltpu.make_async_copy(pv_hbm, vbuf.at[0, 0, 0], ls.at[4]),
        pltpu.make_async_copy(og_hbm, gl.at[g_rows(0)], ls.at[5]),
        pltpu.make_async_copy(w_hbm.at[:, layer(zl)], wl, ls.at[6]),
    ]
    for c in local:
        c.start()
    pl.semaphore_wait(barrier, len(peers))

    started = []

    def remote(src, dst, ssem, rsem, device):
        return pltpu.make_async_remote_copy(
            src_ref=src, dst_ref=dst, send_sem=ssem, recv_sem=rsem, device_id=device, device_id_type=MESH
        )

    def send(*args):
        c = remote(*args)
        c.start()
        started.append(c)

    def landed(dst, ssem, rsem):
        remote(dst, dst, ssem, rsem, other).wait_recv()

    def g_route(kind, c):
        s = 1 if c % 2 == 0 else -1
        return ((0, ydev[s], -s), (0, ydev[-s], s), (s, ydev[-s], 2))[kind]

    def g_send(kind, c):
        ry, to, _ = g_route(kind, c)
        cols = pl.ds(c * CH, CH)
        at = gl.at[g_rows(ry), cols]
        send(og_hbm.at[:, cols] if kind < 2 else at, at, gs.at[kind, c], gr.at[kind, c], to)

    def g_wait(kind, c):
        landed(gl.at[g_rows(g_route(kind, c)[2]), pl.ds(c * CH, CH)], gs.at[kind, c], gr.at[kind, c])

    def g_forward(c):
        g_wait(1, c)
        g_send(2, c)

    def w_rows(stage, rc, part):
        first = stage * 256 + (core if rc == 0 else 1 - core) * 128
        if part is None:
            return pl.ds(pl.multiple_of(first, 128), 128)
        return pl.ds(pl.multiple_of(first + part * 64, 64), 64)

    def w_send(stage):
        for part, to in ((0, pdev), (1, wdev)):
            rows = w_rows(stage, 0, part)
            send(w_hbm.at[rows, layer(1 - zl)], wp.at[rows], wzs.at[stage, part], wzr.at[stage, part], to)

    def w_core(stage):
        for part in range(2):
            landed(wp.at[w_rows(stage, 0, part)], wzs.at[stage, part], wzr.at[stage, part])
        rows = w_rows(stage, 0, None)
        send(wp.at[rows], wp.at[rows], wcs.at[stage], wcr.at[stage], other)

    def w_wait(stage):
        landed(wp.at[w_rows(stage, 1, None)], wcs.at[stage], wcr.at[stage])

    pre = ((0, kbuf, pk_hbm), (1, vbuf, pv_hbm))
    for i, buf, src in pre:
        send(src, buf.at[0, 0, 3], kzs.at[i, 2], kzr.at[i, 2], zdev[1])
        send(src, buf.at[0, 0, 1], kzs.at[i, 0], kzr.at[i, 0], zdev[3])
    w_send(0)
    for i, buf, src in pre:
        for rx in (1, 3, 2):
            send(src, buf.at[rx, 0, 0], kxs.at[i, 0, rx - 1], kxr.at[i, 0, rx - 1], xdev[-rx])
    for c in range(3):
        g_send(0, c)
        g_send(1, c)
    for c in local[:3]:
        c.wait()
    for hd in range(4):
        blk = qb[:, hd * HD : (hd + 1) * HD]
        qs[hd // 2, (hd % 2) * TOK : (hd % 2 + 1) * TOK, :] = blk
        qt[hd // 2, :, (hd % 2) * TOK : (hd % 2 + 1) * TOK] = blk.T

    b0 = len_ref[0, 0]
    b1 = b0 + len_ref[0, 1]
    b2 = b1 + len_ref[0, 2]

    def segment(p):
        return (p >= b0).astype(jnp.int32) + (p >= b1).astype(jnp.int32) + (p >= b2).astype(jnp.int32)

    def weights(kk, hk, cols, mask):
        t = jnp.tanh(dot(kk, qt[hk, :, cols]) * (SCALE / SOFTCAP))
        e = jnp.exp2(t * (SOFTCAP * LOG2E))
        if mask is not None:
            e = jnp.where(mask, e, 0.0)
        return e, e * (1.0 - t * t)

    def partial_sums(e):
        return jnp.sum(e.reshape(e.shape[0] // 8, 8, e.shape[1]), axis=0)

    def doc_forward(hk):
        lsum[hk] = jnp.zeros((8, QW), F32)
        for j in range(4):
            rows = slice(j * HD, (j + 1) * HD)
            lo, hi = j * HD, min(TOK, (j + 3) * HD)
            key = lo + lax.broadcasted_iota(jnp.int32, (HD, hi - lo), 0)
            row = lo + lax.broadcasted_iota(jnp.int32, (HD, hi - lo), 1)
            mask = (key <= row) & (segment(key) == segment(row))
            for g in range(2):
                cols = slice(g * TOK + lo, g * TOK + hi)
                e, s = weights(kd[rows, hk * HD : (hk + 1) * HD], hk, cols, mask)
                lsum[hk, :, cols] += partial_sums(e)
                edoc[hk, rows, cols] = e.astype(BF16)
                sdoc[hk, rows, cols] = s.astype(BF16)
                for a, b in ((0, lo), (hi, TOK)):
                    if a < b:
                        edoc[hk, rows, g * TOK + a : g * TOK + b] = jnp.zeros((HD, b - a), BF16)
                        sdoc[hk, rows, g * TOK + a : g * TOK + b] = jnp.zeros((HD, b - a), BF16)

    def pre_forward(rz):
        def one(hk, carry):
            lanes = pl.ds(pl.multiple_of(hk * HD, HD), HD)
            e, s = weights(kbuf[:, :, rz, :, lanes].reshape(QR, HD), hk, slice(None), None)
            lsum[hk] += partial_sums(e)
            ebuf[hk, :, :, rz] = e.astype(BF16).reshape(4, 2, 64, QW)
            sbuf[hk, :, :, rz] = s.astype(BF16).reshape(4, 2, 64, QW)
            return carry

        lax.fori_loop(0, 2, one, 0)

    def z_landed(rz):
        for i, buf, _ in pre:
            landed(buf.at[0, 0, rz], kzs.at[i, rz - 1], kzr.at[i, rz - 1])

    def x_near(rz):
        for i, buf, _ in pre:
            for rx in (1, 3, 2) if rz == 2 else (1, 3):
                send(buf.at[0, 0, rz], buf.at[rx, 0, rz], kxs.at[i, rz, rx - 1], kxr.at[i, rz, rx - 1], xdev[-rx])

    def x_landed(i, rx, rz):
        landed(pre[i][1].at[rx, 0, rz], kxs.at[i, rz, rx - 1], kxr.at[i, rz, rx - 1])

    def x_pass(rz):
        for i, got, to in ((0, 3, 1), (1, 1, -1)):
            x_landed(i, got, rz)
            buf = pre[i][1]
            send(buf.at[got, 0, rz], buf.at[2, 0, rz], kxs.at[i, rz, 1], kxr.at[i, rz, 1], xdev[to])

    def core_send(rz):
        for i, buf, _ in pre:
            for rx in (1, 3, 2):
                if rz in (0, 2) or rx == 2 or rx == (1, 3)[i]:
                    x_landed(i, rx, rz)
            send(buf.at[:, 0, rz], buf.at[:, 1, rz], kcs.at[i, rz], kcr.at[i, rz], other)

    def core_wait(rz):
        for i, buf, _ in pre:
            landed(buf.at[:, 1, rz], kcs.at[i, rz], kcr.at[i, rz])

    doc_forward(0)
    doc_forward(1)

    def project(w, n):
        return dot(w, gl[:, n * 256 : (n + 1) * 256])

    def g_last(n):
        for c in (2 * n, 2 * n + 1):
            g_wait(0, c)
            g_wait(2, c)

    def own(n):
        hgt[:, n * 256 : (n + 1) * 256] = project(wl[...], n)

    def partner(n, stage):
        rows = pl.ds(stage * 256, 256)
        cols = pl.ds(n * 256, 256)
        hs[rows, cols] = project(wp[rows, :], n).astype(BF16)
        send(hs.at[rows, cols], hr.at[rows, cols], hss.at[n, stage], hrs.at[n, stage], pdev)

    g_forward(0)
    for c in local[3:5]:
        c.wait()
    core_send(0)
    for rz in (1, 3):
        z_landed(rz)
    for i, buf, _ in pre:
        send(buf.at[0, 0, 3 - 2 * i], buf.at[0, 0, 2], kzs.at[i, 1], kzr.at[i, 1], zdev[1 + 2 * i])
    w_send(1)
    for rz in (1, 3):
        x_near(rz)
    g_forward(1)
    g_send(0, 3)
    g_send(1, 3)
    core_wait(0)
    pre_forward(0)
    x_pass(1)
    x_pass(3)
    g_forward(2)
    w_core(0)
    core_send(1)
    core_send(3)
    g_last(0)
    for c in local[5:]:
        c.wait()
    w_wait(0)
    partner(0, 0)
    g_forward(3)
    z_landed(2)
    x_near(2)
    own(0)
    w_core(1)
    core_wait(1)
    pre_forward(1)
    w_wait(1)
    partner(0, 1)
    g_last(1)
    partner(1, 0)
    partner(1, 1)
    core_send(2)
    core_wait(3)
    pre_forward(3)
    own(1)
    core_wait(2)
    pre_forward(2)
    for hk in range(2):
        lanes = slice(hk * HD, (hk + 1) * HD)
        vv = vbuf[:, :, :, :, lanes].reshape(PRE, HD)
        ot[hk] = dot(vv, ebuf[hk].reshape(PRE, QW), ((0,), (0,))) + dot(vd[:, lanes], edoc[hk], ((0,), (0,)))
    for n in range(2):
        cols = pl.ds(n * 256, 256)
        for stage in range(2):
            rows = pl.ds(stage * 256, 256)
            landed(hr.at[rows, cols], hss.at[n, stage], hrs.at[n, stage])
        hgt[:, cols] += hr[:, cols].astype(F32)

    for hd in range(4):
        hk, cols = hd // 2, slice((hd % 2) * TOK, (hd % 2 + 1) * TOK)
        g = hgt[hd * HD : (hd + 1) * HD, :].astype(BF16).astype(F32)
        inv = 1.0 / jnp.sum(lsum[hk, :, cols], axis=0, keepdims=True)
        scaled = (g * inv).astype(BF16)
        drow[hk, :, cols] = jnp.sum(g * ot[hk, :, cols], axis=0, keepdims=True) * (inv * inv)
        dot_t[hk, :, cols] = scaled
        dos[hk, cols, :] = scaled.T

    def put_terms(a, hk, rz, t):
        t = t.astype(BF16).reshape(4, 2, 64, HD)
        for rc in range(2):
            pb[rz, a, rc, :, :, hk * HD : (hk + 1) * HD] = t[:, rc]

    def dv_block(rz):
        for hk in range(2):
            put_terms(0, hk, rz, dot(ebuf[hk, :, :, rz].reshape(QR, QW), dos[hk]))
        pair_send(rz, 0)

    def logit_grads(vv, hk, s, cols):
        dp = dot(vv, dot_t[hk, :, cols]) - drow[hk, :, cols]
        return (s.astype(F32) * dp).astype(BF16)

    def dk_block(rz):
        for hk in range(2):
            vv = vbuf[:, :, rz, :, hk * HD : (hk + 1) * HD].reshape(QR, HD)
            for n in range(2):
                cols = slice(n * TOK, (n + 1) * TOK)
                ds = logit_grads(vv, hk, sbuf[hk, :, :, rz, :, cols].reshape(QR, TOK), cols)
                sbuf[hk, :, :, rz, :, cols] = ds.reshape(4, 2, 64, TOK)
            put_terms(1, hk, rz, dot(sbuf[hk, :, :, rz].reshape(QR, QW), qs[hk]) * SCALE)
        pair_send(rz, 1)

    def pair_send(rz, a):
        send(pb.at[rz, a, 1], pr.at[rz, a], ps.at[rz, a], prs.at[rz, a], other)

    def pair_sum(rz, a, rx):
        return pb[rz, a, 0, rx].astype(F32) + pr[rz, a, rx].astype(F32)

    def pair_wait(rz, a):
        landed(pr.at[rz, a], ps.at[rz, a], prs.at[rz, a])

    def z_first(rz):
        n = rz // 2
        pair_wait(rz, 0)
        for rx in range(4):
            vs[n, rx] = pair_sum(rz, 0, rx).astype(BF16)
        send(vs.at[n], vr.at[n], vss.at[n], vrs.at[n], zdev[rz])

    def stay(a, rx):
        t = pair_sum(0, a, rx)
        return t if a else t + vr[0, rx].astype(F32) + vr[1, rx].astype(F32)

    def x_send(rz, a):
        pair_wait(rz, a)
        if rz == 0 and a == 0:
            for n in range(2):
                landed(vr.at[n], vss.at[n], vrs.at[n])
        for rx in (2, 1, 3):
            n = rx - 1
            t = pair_sum(rz, a, rx) if rz else stay(a, rx)
            xs[rz, a, n] = t.astype(BF16)
            send(xs.at[rz, a, n], xr.at[rz, a, n], xss.at[rz, a, n], xrs.at[rz, a, n], xdev[rx - 4])

    def x_total(rz, a):
        t = pair_sum(rz, a, 0) if rz else stay(a, 0)
        for n in range(3):
            landed(xr.at[rz, a, n], xss.at[rz, a, n], xrs.at[rz, a, n])
            t = t + xr[rz, a, n].astype(F32)
        if rz:
            zs[rz - 1, a] = t.astype(BF16)
            send(zs.at[rz - 1, a], zr.at[rz - 1, a], zss.at[rz - 1, a], zrs.at[rz - 1, a], zdev[rz])
        else:
            tacc[a] = t

    outs = []

    def put(src, dst, n):
        c = pltpu.make_async_copy(src, dst, osem.at[n])
        c.start()
        outs.append(c)

    def z_total(a, out, dst):
        t = tacc[a]
        for n in (1, 0, 2) if a else (1,):
            landed(zr.at[n, a], zss.at[n, a], zrs.at[n, a])
            t = t + zr[n, a].astype(F32)
        out[...] = t.astype(BF16)
        put(out, dst, a)

    dv_block(1)
    dv_block(3)
    dv_block(2)
    z_first(1)
    dk_block(2)
    z_first(3)
    x_send(2, 0)
    dk_block(1)
    x_send(2, 1)
    dk_block(3)
    x_send(1, 1)
    dv_block(0)
    x_send(3, 1)
    dk_block(0)
    x_total(2, 0)
    x_total(2, 1)

    def doc_backward(hk):
        lanes = slice(hk * HD, (hk + 1) * HD)
        for n in range(2):
            cols = slice(n * TOK, (n + 1) * TOK)
            sdoc[hk, :, cols] = logit_grads(vd[:, lanes], hk, sdoc[hk, :, cols], cols)
        odk[:, lanes] = (dot(sdoc[hk], qs[hk]) * SCALE).astype(BF16)
        odv[:, lanes] = dot(edoc[hk], dos[hk]).astype(BF16)

    doc_backward(0)
    x_send(0, 1)
    x_total(1, 1)
    x_total(3, 1)
    x_send(0, 0)
    doc_backward(1)
    put(odk, dk_hbm, 2)
    put(odv, dv_hbm, 3)

    for hk in range(2):
        lanes = slice(hk * HD, (hk + 1) * HD)
        kk = kbuf[:, :, :, :, lanes].reshape(PRE, HD)
        t = dot(kk, sbuf[hk].reshape(PRE, QW), ((0,), (0,))) + dot(kd[:, lanes], sdoc[hk], ((0,), (0,)))
        for g in range(2):
            hd = hk * 2 + g
            odq[:, hd * HD : (hd + 1) * HD] = (t[:, g * TOK : (g + 1) * TOK] * SCALE).astype(BF16).T
    put(odq, dq_hbm, 4)
    x_total(0, 1)
    z_total(1, opk, pdk_hbm)
    x_total(0, 0)
    z_total(0, opv, pdv_hbm)
    for c in started:
        c.wait_send()
    for c in outs:
        c.wait()


def finish(*refs):
    ins, outs, held, sem = refs[:5], refs[5:10], refs[10:15], refs[15]
    into = [pltpu.make_async_copy(a, b, sem.at[0, i]) for i, (a, b) in enumerate(zip(ins, held))]
    back = [pltpu.make_async_copy(a, b, sem.at[1, i]) for i, (a, b) in enumerate(zip(held, outs))]
    for c in into:
        c.start()
    for a, b in zip(into, back):
        a.wait()
        b.start()
    for c in back:
        c.wait()


def on_device(queries, keys, values, prefix_keys, prefix_values, out_grad, out_weight, doc_lengths):
    sd = jax.ShapeDtypeStruct
    hbm = pl.BlockSpec(memory_space=pl.ANY)
    vm = pltpu.VMEM
    dma = pltpu.SemaphoreType.DMA
    shapes = (
        sd((TOK, 512), BF16),
        sd((TOK, 256), BF16),
        sd((TOK, 256), BF16),
        sd((64, 256), BF16),
        sd((64, 256), BF16),
    )
    grads = pl.pallas_call(
        kernel,
        out_shape=shapes,
        in_specs=[pl.BlockSpec(memory_space=pltpu.SMEM)] + [hbm] * 7,
        out_specs=(hbm,) * 5,
        scratch_shapes=[
            vm((TOK, 512), BF16),
            vm((TOK, 256), BF16),
            vm((TOK, 256), BF16),
            vm((LAY, TOK), BF16),
            vm((512, LAY), BF16),
            vm((512, LAY), BF16),
            vm((512, TOK), BF16),
            vm((512, TOK), BF16),
            vm((4, 2, 4, 64, 256), BF16),
            vm((4, 2, 4, 64, 256), BF16),
            vm((2, 4, 2, 4, 64, QW), BF16),
            vm((2, 4, 2, 4, 64, QW), BF16),
            vm((2, TOK, QW), BF16),
            vm((2, TOK, QW), BF16),
            vm((2, HD, QW), BF16),
            vm((2, QW, HD), BF16),
            vm((2, HD, QW), BF16),
            vm((2, QW, HD), BF16),
            vm((2, HD, QW), F32),
            vm((2, 8, QW), F32),
            vm((2, 1, QW), F32),
            vm((512, TOK), F32),
            vm((4, 2, 2, 4, 64, 256), BF16),
            vm((4, 2, 4, 64, 256), BF16),
            vm((2, 4, 64, 256), BF16),
            vm((2, 4, 64, 256), BF16),
            vm((4, 2, 3, 64, 256), BF16),
            vm((4, 2, 3, 64, 256), BF16),
            vm((2, 64, 256), F32),
            vm((3, 2, 64, 256), BF16),
            vm((3, 2, 64, 256), BF16),
            vm((TOK, 512), BF16),
            vm((TOK, 256), BF16),
            vm((TOK, 256), BF16),
            vm((64, 256), BF16),
            vm((64, 256), BF16),
            dma((7,)),
            dma((3, NC)),
            dma((3, NC)),
            dma((2, 2)),
            dma((2, 2)),
            dma((2, 2)),
            dma((2, 2)),
            dma((2,)),
            dma((2,)),
            dma((2, 3)),
            dma((2, 3)),
            dma((2, 4, 3)),
            dma((2, 4, 3)),
            dma((2, 4)),
            dma((2, 4)),
            dma((4, 2)),
            dma((4, 2)),
            dma((2,)),
            dma((2,)),
            dma((4, 2, 3)),
            dma((4, 2, 3)),
            dma((3, 2)),
            dma((3, 2)),
            dma((5,)),
        ],
        compiler_params=pltpu.CompilerParams(
            collective_id=0, has_side_effects=True, vmem_limit_bytes=60 * 1024 * 1024
        ),
    )(doc_lengths, queries, keys, values, prefix_keys, prefix_values, out_grad.T, out_weight)
    return pl.pallas_call(
        finish,
        out_shape=shapes,
        in_specs=[hbm] * 5,
        out_specs=(hbm,) * 5,
        scratch_shapes=[vm(s.shape, s.dtype) for s in shapes] + [dma((2, 5))],
    )(*grads)


def solution(mesh):
    return jax.shard_map(
        on_device,
        mesh=mesh,
        in_specs=(P("docs", "heads"),) * 6 + (P("heads", None), P("docs", None)),
        out_specs=(P("docs", "heads"),) * 5,
        check_vma=False,
    )
```
